32 devices in a mesh: row: 4 (over y, core), col: 4 (over z), dp: 2 (over x).
Axes of the slice: x: 2, y: 2, z: 4, core: 2. Of those that a mesh axis runs over, the one named last changes fastest.
Arguments:
- pair: bfloat16 [2, 64, 512, 512], P('dp', None, 'row', 'col'), may hold values from -120 to 120
- cotangent: bfloat16 [2, 64, 512, 512], P('dp', None, 'row', 'col'), may hold values from -6 to 6
- chain: int32 [2, 512], P('dp'), may hold values from 0 to 3, never falling along the last dimension, each value on 1 to 256 neighbouring positions
- dilation: int32 [2], replicated, may hold values from 1 to 8, as said below
- w_one: bfloat16 [9, 64, 64], replicated, may hold values from -0.25 to 0.25
- w_two: bfloat16 [9, 64, 64], replicated, may hold values from -0.25 to 0.25
- gain_one: float32 [64], replicated, may hold values from 0.25 to 1.75
- gain_two: float32 [64], replicated, may hold values from 0.25 to 1.75
- inter_bias: float32 [64], replicated, may hold values from -4 to 4
Outputs:
- grad_w_one: float32 [9, 64, 64], replicated
- grad_w_two: float32 [9, 64, 64], replicated
- grad_gain_one: float32 [64], replicated
- grad_gain_two: float32 [64], replicated
- grad_inter: float32 [64], replicated
- loss: float32 [], replicated
The draws below stay inside these ranges and needn't reach their ends.
Inputs may be any that keep to these rules, and one draw needn't show every extreme that they name: `dilation`: each entry is 1, 2, 4 or 8, and at least one entry is 8. chain numbers never fall along a complex's residues; each of the 4 chains has at most 256 residues.
All inputs are finite; a program needn't handle non-finite values.
Results may differ from the reference program's by a relative error of at most 0.0071.
Values may be sent and summed in bfloat16 or wider, within the bound.
A program may use at most 128 MiB of HBM per device.

```python
import math
import jax
import jax.numpy as jnp
import numpy as np
from jax import lax

C = 64
TAPS = 9
L = 512
BATCH = 2


def draw_pair(key, part):
    keys = jax.random.split(key, 4)
    ramp = jnp.arange(L, dtype=jnp.float32) / (L - 1)
    row_scale = jnp.exp(ramp * jnp.log(3.0) + jax.random.uniform(keys[1], (L,), jnp.float32, 0.0, jnp.log(3.3)))
    col_scale = jnp.exp(ramp * jnp.log(3.0) + jax.random.uniform(keys[2], (L,), jnp.float32, 0.0, jnp.log(3.3)))
    chan_scale = jnp.exp(jax.random.uniform(keys[3], (C,), jnp.float32, jnp.log(0.5), jnp.log(2.0)))
    base = jnp.clip(jax.random.normal(keys[0], (BATCH, C, L, L), jnp.float32), -6.0, 6.0)
    scaled = base * chan_scale[None, :, None, None] * row_scale[None, None, :, None] * col_scale[None, None, None, :] * 0.1
    return scaled.astype(jnp.bfloat16)


def draw_dilation(key, part):
    first, second = jax.random.split(key)
    which = jax.random.randint(first, (), 0, 2)
    power = jax.random.randint(second, (), 0, 3).astype(jnp.int32)
    other = jnp.left_shift(jnp.int32(1), power)
    return jnp.where(jnp.arange(2) == which, jnp.int32(8), other).astype(jnp.int32)


def levels(own_key, dims, pieces, smallest, high):
    factor_of, own = 1.0, jax.random.fold_in(own_key, 6)
    for dim, blocks in pieces:
        steps = jnp.exp(jax.random.uniform(jax.random.fold_in(own, dim), (blocks,), jnp.float32, smallest / len(pieces), high / len(pieces)))
        factor_of = factor_of * jnp.repeat(steps, dims[dim] // blocks).reshape([-1 if axis == dim else 1 for axis in range(len(dims))])
    return factor_of


def split_up(count, total, limit, lean):
    weights = [(1 << 20) // math.isqrt(standing ** lean) + 1 for standing in range(2, count + 1)]
    surplus, holding = total - limit - (count - 1), [1] * (count - 1)
    while surplus > 0:
        movable = [i for i in range(count - 1) if holding[i] < limit]
        pool, left = sum([weights[i] for i in movable]), surplus
        for i in movable:
            addition = min(limit - holding[i], max(1, left * weights[i] // pool), surplus)
            holding[i] = holding[i] + addition
            surplus = surplus - addition
    return np.array([limit] + holding)


def ragged_sizes(stream_key, count, total, reach, slope):
    if count == 2:
        one = jax.random.randint(stream_key, (), max(1, total - reach), min(reach, total - 1) + 1)
        return jnp.stack([one, total - one])
    tallies = jnp.asarray(split_up(count, total, reach, slope), jnp.int32)
    twos = (count - 1) // 2
    source_of, taker = tallies[1:1 + 2 * twos:2], tallies[2:2 + 2 * twos:2]
    slack = jnp.minimum(source_of - 1, reach - taker)
    moved = jax.random.randint(jax.random.fold_in(stream_key, 1), (twos,), 0, 1 << 20) % (slack + 1)
    tallies = tallies.at[1:1 + 2 * twos:2].set(source_of - moved).at[2:2 + 2 * twos:2].set(taker + moved)
    return tallies[jax.random.permutation(jax.random.fold_in(stream_key, 2), count)]


def noise(rng, shape, scale, bound, shards=(), kind=jnp.bfloat16):
    values = scale * jax.random.normal(rng, shape, jnp.float32)
    if shards:
        values = values * levels(rng, shape, shards, -0.22, 0.18)
    return jnp.clip(values, -bound, bound).astype(kind)


def setup_inputs(seed: int = 0) -> dict:
    arg_keys = jax.random.split(jax.random.key(seed), 10)
    pair = draw_pair(jax.random.fold_in(arg_keys[9], 71), 0)
    cotangent = noise(arg_keys[1], (BATCH, C, L, L), 1.0, 6.0, ((0, 2), (2, 4), (3, 4)))
    chain = jax.vmap(lambda own: jnp.searchsorted(jnp.cumsum(ragged_sizes(own, 4, L, L // 2, 0)), jnp.arange(L), side="right"))(jax.random.split(arg_keys[2], BATCH)).reshape((BATCH, L)).astype(jnp.int32)
    dilation = draw_dilation(jax.random.fold_in(arg_keys[9], 71), 0)
    w_one = noise(arg_keys[4], (TAPS, C, C), (TAPS * C) ** -0.5, 0.25)
    w_two = noise(arg_keys[5], (TAPS, C, C), (TAPS * C) ** -0.5, 0.25)
    gain_one = jnp.clip(1.0 + 0.15 * jax.random.normal(arg_keys[6], (C,), jnp.float32), 0.25, 1.75)
    gain_two = jnp.clip(1.0 + 0.15 * jax.random.normal(arg_keys[7], (C,), jnp.float32), 0.25, 1.75)
    inter_bias = noise(arg_keys[8], (C,), 1.0, 4.0, (), jnp.float32)
    return dict(pair=pair, cotangent=cotangent, chain=chain, dilation=dilation, w_one=w_one, w_two=w_two, gain_one=gain_one, gain_two=gain_two, inter_bias=inter_bias)


kernel_reach = 8
eps = 1e-05

def elu(z):
    return jnp.where(z > 0, z, jnp.exp(jnp.minimum(z, 0.0)) - 1.0)

def elu_slope(z):
    return jnp.where(z > 0, 1.0, jnp.exp(jnp.minimum(z, 0.0)))

def kernel_tap_window(padded_input, first, second, input_shape):
    zero = jnp.int32(0)
    return lax.dynamic_slice(padded_input, (zero, first.astype(jnp.int32), second.astype(jnp.int32)), input_shape)

def widen(values):
    return jnp.pad(values, ((0, 0), (kernel_reach, kernel_reach), (kernel_reach, kernel_reach)))

def dilated_convolve(activation_map, kernel_weights, dilation_rate):
    chans = activation_map.shape[0]
    padded_input = widen(activation_map)
    total = jnp.zeros((chans, activation_map.shape[1] * activation_map.shape[2]), jnp.float32)
    for step in range(9):
        upper_triangle, left_padding = (step // 3 - 1, step % 3 - 1)
        window_slice = kernel_tap_window(padded_input, kernel_reach + dilation_rate * upper_triangle, kernel_reach + dilation_rate * left_padding, activation_map.shape)
        total = total + jnp.dot(kernel_weights[step], window_slice.reshape(chans, -1), preferred_element_type=jnp.float32)
    return total.reshape(activation_map.shape)

def convolve_backward(output_gradient, kernel_weights, dilation_rate):
    chans = output_gradient.shape[0]
    padded_input = widen(output_gradient)
    total = jnp.zeros((chans, output_gradient.shape[1] * output_gradient.shape[2]), jnp.float32)
    for step in range(9):
        upper_triangle, left_padding = (step // 3 - 1, step % 3 - 1)
        window_slice = kernel_tap_window(padded_input, kernel_reach - dilation_rate * upper_triangle, kernel_reach - dilation_rate * left_padding, output_gradient.shape)
        total = total + jnp.dot(kernel_weights[step].T, window_slice.reshape(chans, -1), preferred_element_type=jnp.float32)
    return total.reshape(output_gradient.shape)

def kernel_weight_gradient(output_gradient, activation_map, dilation_rate):
    chans = activation_map.shape[0]
    padded_input = widen(activation_map)
    flat = output_gradient.reshape(chans, -1)
    result = []
    for step in range(9):
        upper_triangle, left_padding = (step // 3 - 1, step % 3 - 1)
        window_slice = kernel_tap_window(padded_input, kernel_reach + dilation_rate * upper_triangle, kernel_reach + dilation_rate * left_padding, activation_map.shape)
        result.append(lax.dot_general(flat, window_slice.reshape(chans, -1), (((1,), (1,)), ((), ())), preferred_element_type=jnp.float32))
    return jnp.stack(result)

def normalize(values):
    count = values.shape[1] * values.shape[2]
    mean = lax.optimization_barrier(jnp.sum(values, axis=(1, 2))) / count
    centred = values - mean[:, None, None]
    var = lax.optimization_barrier(jnp.sum(centred * centred, axis=(1, 2))) / count
    return (centred * lax.rsqrt(var + eps)[:, None, None], var)

def reference(pair, cotangent, chain, dilation, w_one, w_two, gain_one, gain_two, inter_bias):

    def one_complex(items):
        tile, cot, ids = items
        side = tile.shape[1]
        count = side * side
        sym = ((tile.astype(jnp.float32) + jnp.swapaxes(tile, 1, 2).astype(jnp.float32)) * 0.5).astype(jnp.bfloat16)
        wide = sym.astype(jnp.float32)
        norm_one, var_one = normalize(wide)
        z_one = gain_one[:, None, None] * norm_one
        act_one = elu(z_one).astype(jnp.bfloat16)
        cross = (ids[:, None] != ids[None, :]).astype(jnp.float32)
        hid = dilated_convolve(act_one, w_one, dilation[0]) + inter_bias[:, None, None] * cross[None]
        norm_two, var_two = normalize(hid)
        z_two = gain_two[:, None, None] * norm_two
        act_two = elu(z_two).astype(jnp.bfloat16)
        upd = dilated_convolve(act_two, w_two, dilation[1])
        cot_wide = cot.astype(jnp.float32)
        loss = jnp.sum((wide + upd) * cot_wide) / side
        g_upd = (cot_wide / side).astype(jnp.bfloat16)
        grad_two = kernel_weight_gradient(g_upd, act_two, dilation[1])
        d_act_two = convolve_backward(g_upd, w_two, dilation[1])
        d_z_two = d_act_two * elu_slope(z_two)
        grad_g_two = lax.optimization_barrier(jnp.sum(d_z_two * norm_two, axis=(1, 2)))
        d_norm_two = d_z_two * gain_two[:, None, None]
        mean_a = lax.optimization_barrier(jnp.sum(d_norm_two, axis=(1, 2))) / count
        mean_b = lax.optimization_barrier(jnp.sum(d_norm_two * norm_two, axis=(1, 2))) / count
        d_hid = (d_norm_two - mean_a[:, None, None] - norm_two * mean_b[:, None, None]) * lax.rsqrt(var_two + eps)[:, None, None]
        grad_int = lax.optimization_barrier(jnp.sum(d_hid * cross[None], axis=(1, 2)))
        d_hid_low = d_hid.astype(jnp.bfloat16)
        grad_one = kernel_weight_gradient(d_hid_low, act_one, dilation[0])
        d_act_one = convolve_backward(d_hid_low, w_one, dilation[0])
        grad_g_one = lax.optimization_barrier(jnp.sum(d_act_one * elu_slope(z_one) * norm_one, axis=(1, 2)))
        return (grad_one, grad_two, grad_g_one, grad_g_two, grad_int, loss)
    outs = lax.map(one_complex, (pair, cotangent, chain))
    return (lax.optimization_barrier(jnp.sum(outs[0], axis=0)), lax.optimization_barrier(jnp.sum(outs[1], axis=0)), lax.optimization_barrier(jnp.sum(outs[2], axis=0)), lax.optimization_barrier(jnp.sum(outs[3], axis=0)), lax.optimization_barrier(jnp.sum(outs[4], axis=0)), lax.optimization_barrier(jnp.sum(outs[5], axis=0)))
```

```python
import functools

import jax
import jax.numpy as jnp
from jax import lax
from jax.experimental import pallas as pl
from jax.experimental.pallas import tpu as pltpu
from jax.sharding import PartitionSpec as P

reach = 8
eps = 1e-05
f32 = jnp.float32
bf16 = jnp.bfloat16
MESH = pl.DeviceIdType.MESH
vmem = pl.BlockSpec(memory_space=pltpu.VMEM)
smem = pl.BlockSpec(memory_space=pltpu.SMEM)
anyspace = pl.BlockSpec(memory_space=pl.ANY)
LIMIT = 56 * 1024 * 1024


def shape(dims, dtype):
    return jax.ShapeDtypeStruct(dims, dtype)


def lanes(chans=64, width=128):
    return lax.broadcasted_iota(jnp.int32, (chans, width), 1)


def pack_edges(rows, chans, side):
    group = lanes(chans, side) // reach
    low = jnp.zeros((chans, side), f32)
    high = jnp.zeros((chans, side), f32)
    for j, row in enumerate(rows):
        low = jnp.where(group == j, row if j == 0 else pltpu.roll(row, 8 * j, 1), low)
        shift = (8 * j + 8) % side
        high = jnp.where(group == j, row if shift == 0 else pltpu.roll(row, shift, 1), high)
    return low.astype(bf16), high.astype(bf16)


def as_columns(columns, chans, side):
    lane = lanes(chans, side)
    tile = jnp.zeros((chans, side), f32)
    for k, values in enumerate(columns):
        tile = jnp.where(lane == k, jnp.sum(values, axis=1, keepdims=True), tile)
    return tile


def edges_kernel(x_ref, low_ref, high_ref):
    side, chans = x_ref.shape[0], x_ref.shape[1]

    def body(k, carry):
        rows = [x_ref[16 * k + j].astype(f32) for j in range(16)]
        low_ref[k], high_ref[k] = pack_edges(rows, chans, side)
        return carry

    lax.fori_loop(0, side // 16, body, 0)


def sym_kernel(x_ref, m_ref, cot_ref, sym_ref, low_ref, high_ref, stat_ref):
    side, chans = x_ref.shape[0], x_ref.shape[1]

    def body(k, carry):
        one, two, three = carry
        rows = []
        for j in range(16):
            p = 16 * k + j
            sym = ((x_ref[p].astype(f32) + m_ref[p].astype(f32)) * 0.5).astype(bf16)
            sym_ref[p] = sym
            wide = sym.astype(f32)
            rows.append(wide)
            one = one + wide
            two = two + wide * wide
            three = three + wide * cot_ref[p].astype(f32)
        low_ref[k], high_ref[k] = pack_edges(rows, chans, side)
        return one, two, three

    zero = jnp.zeros((chans, side), f32)
    sums = lax.fori_loop(0, side // 16, body, (zero, zero, zero))
    stat_ref[...] = as_columns(sums, chans, side)


def halo_body(x_ref, low_ref, high_ref, top_ref, bot_ref, left_ref, right_ref, send, recv):
    rows, cols = lax.axis_size("row"), lax.axis_size("col")
    r, c = lax.axis_index("row"), lax.axis_index("col")
    up, down = lax.rem(r + rows - 1, rows), lax.rem(r + 1, rows)
    lef, rig = lax.rem(c + cols - 1, cols), lax.rem(c + 1, cols)
    side, blocks = x_ref.shape[0], low_ref.shape[0]
    moves = [
        (high_ref, left_ref.at[pl.ds(1, blocks)], r, rig),
        (low_ref, right_ref.at[pl.ds(1, blocks)], r, lef),
        (x_ref.at[pl.ds(side - reach, reach)], top_ref, down, c),
        (x_ref.at[pl.ds(0, reach)], bot_ref, up, c),
        (high_ref.at[pl.ds(blocks - 1, 1)], left_ref.at[pl.ds(0, 1)], down, rig),
        (high_ref.at[pl.ds(0, 1)], left_ref.at[pl.ds(blocks + 1, 1)], up, rig),
        (low_ref.at[pl.ds(blocks - 1, 1)], right_ref.at[pl.ds(0, 1)], down, lef),
        (low_ref.at[pl.ds(0, 1)], right_ref.at[pl.ds(blocks + 1, 1)], up, lef),
    ]
    return [
        pltpu.make_async_remote_copy(
            src_ref=src,
            dst_ref=dst,
            send_sem=send.at[n],
            recv_sem=recv.at[n],
            device_id={"row": to_row, "col": to_col},
            device_id_type=MESH,
        )
        for n, (src, dst, to_row, to_col) in enumerate(moves)
    ]


def halo_kernel(x_ref, low_ref, high_ref, top_ref, bot_ref, left_ref, right_ref, send, recv):
    rows, cols = lax.axis_size("row"), lax.axis_size("col")
    r, c = lax.axis_index("row"), lax.axis_index("col")
    barrier = pltpu.get_barrier_semaphore()
    for a in (-1, 0, 1):
        for b in (-1, 0, 1):
            if a or b:
                pl.semaphore_signal(
                    barrier,
                    inc=1,
                    device_id={
                        "row": lax.rem(r + rows + a, rows),
                        "col": lax.rem(c + cols + b, cols),
                    },
                    device_id_type=MESH,
                )
    pl.semaphore_wait(barrier, 8)
    copies = halo_body(x_ref, low_ref, high_ref, top_ref, bot_ref, left_ref, right_ref, send, recv)
    for copy in copies:
        copy.start()
    for copy in copies:
        copy.wait()


def halo(x, low, high, number):
    side, chans, width = x.shape
    blocks = low.shape[0]
    return pl.pallas_call(
        halo_kernel,
        name="halo",
        out_shape=[
            shape((reach, chans, width), bf16),
            shape((reach, chans, width), bf16),
            shape((blocks + 2, chans, width), bf16),
            shape((blocks + 2, chans, width), bf16),
        ],
        in_specs=[anyspace] * 3,
        out_specs=[anyspace] * 4,
        scratch_shapes=[pltpu.SemaphoreType.DMA((8,)), pltpu.SemaphoreType.DMA((8,))],
        compiler_params=pltpu.CompilerParams(collective_id=number, has_side_effects=True),
    )(x, low, high)


def peer_of(index, cols, depth):
    return {
        "row": index // (cols * depth),
        "col": lax.rem(index // depth, cols),
        "dp": lax.rem(index, depth),
    }


def greet(barrier, me, count, peer):
    def body(step, carry):
        to = lax.rem(me + step, count)
        pl.semaphore_signal(barrier, inc=1, device_id=peer(to), device_id_type=MESH)
        return carry

    lax.fori_loop(1, count, body, 0)
    pl.semaphore_wait(barrier, count - 1)


def stats_kernel(x_ref, out_ref, own, slots, send, recv):
    rows, cols = lax.axis_size("row"), lax.axis_size("col")
    count = rows * cols
    me = lax.axis_index("row") * cols + lax.axis_index("col")
    chans = x_ref.shape[0]

    def peer(index):
        return {"row": index // cols, "col": lax.rem(index, cols)}

    greet(pltpu.get_barrier_semaphore(), me, count, peer)
    own[...] = x_ref[...].T[0:8, :]

    def copy_to(step):
        return pltpu.make_async_remote_copy(
            src_ref=own,
            dst_ref=slots.at[me],
            send_sem=send.at[step],
            recv_sem=recv.at[me],
            device_id=peer(lax.rem(me + step, count)),
            device_id_type=MESH,
        )

    def copy_from(step):
        source = lax.rem(me + step, count)
        return pltpu.make_async_remote_copy(
            src_ref=own,
            dst_ref=slots.at[source],
            send_sem=send.at[step],
            recv_sem=recv.at[source],
            device_id=peer(source),
            device_id_type=MESH,
        )

    def start(step, carry):
        copy_to(step).start()
        return carry

    def land(step, carry):
        copy_to(step).wait_send()
        copy_from(step).wait_recv()
        return carry

    slots[me] = own[...]
    lax.fori_loop(1, count, start, 0)
    lax.fori_loop(1, count, land, 0)
    total = jnp.sum(slots[...], axis=0)
    filled = jnp.concatenate([total, jnp.zeros((x_ref.shape[1] - 8, chans), f32)], axis=0)
    out_ref[...] = filled.T


def all_stats(tile, number):
    count = lax.axis_size("row") * lax.axis_size("col")
    chans = tile.shape[0]
    return pl.pallas_call(
        stats_kernel,
        name="stats",
        out_shape=shape(tile.shape, f32),
        in_specs=[vmem],
        out_specs=vmem,
        scratch_shapes=[
            pltpu.VMEM((8, chans), f32),
            pltpu.VMEM((count, 8, chans), f32),
            pltpu.SemaphoreType.DMA((count,)),
            pltpu.SemaphoreType.DMA((count,)),
        ],
        compiler_params=pltpu.CompilerParams(collective_id=number, has_side_effects=True),
    )(tile)


def total_kernel(x_ref, out_ref, slots, send, recv, send_two, recv_two):
    rows, cols, depth = lax.axis_size("row"), lax.axis_size("col"), lax.axis_size("dp")
    count = rows * cols * depth
    me = (lax.axis_index("row") * cols + lax.axis_index("col")) * depth + lax.axis_index("dp")
    peer = functools.partial(peer_of, cols=cols, depth=depth)
    greet(pltpu.get_barrier_semaphore(), me, count, peer)

    def scatter(step, source):
        to = lax.rem(me + step, count)
        return pltpu.make_async_remote_copy(
            src_ref=x_ref.at[to],
            dst_ref=slots.at[source],
            send_sem=send.at[step],
            recv_sem=recv.at[source],
            device_id=peer(to),
            device_id_type=MESH,
        )

    def gather(step, source):
        to = lax.rem(me + step, count)
        return pltpu.make_async_remote_copy(
            src_ref=out_ref.at[source],
            dst_ref=out_ref.at[source],
            send_sem=send_two.at[step],
            recv_sem=recv_two.at[source],
            device_id=peer(to),
            device_id_type=MESH,
        )

    def run(make):
        def start(step, carry):
            make(step, me).start()
            return carry

        def land(step, carry):
            make(step, me).wait_send()
            make(step, lax.rem(me + step, count)).wait_recv()
            return carry

        lax.fori_loop(1, count, start, 0)
        lax.fori_loop(1, count, land, 0)

    slots[me] = x_ref[me]
    run(scatter)
    out_ref[me] = jnp.sum(slots[...], axis=0)
    run(gather)


def grand_total(flat, number):
    count = lax.axis_size("row") * lax.axis_size("col") * lax.axis_size("dp")
    rows = flat.shape[0]
    each = -(-rows // (8 * count)) * 8
    padded = jnp.pad(flat, ((0, each * count - rows), (0, 0))).reshape(count, each, 128)
    out = pl.pallas_call(
        total_kernel,
        name="total",
        out_shape=shape(padded.shape, f32),
        in_specs=[vmem],
        out_specs=vmem,
        scratch_shapes=[pltpu.VMEM(padded.shape, f32)] + [pltpu.SemaphoreType.DMA((count,))] * 4,
        compiler_params=pltpu.CompilerParams(
            collective_id=number, has_side_effects=True, vmem_limit_bytes=LIMIT
        ),
    )(padded)
    return out.reshape(each * count, 128)[:rows]


def stack_shifts(centre, left, right, out_ref, dil):
    height, chans, side = centre.shape
    lane = lanes(chans, side)

    def body(row, carry):
        block, j = (row + reach) // 16, lax.rem(row + reach, 16)
        x = centre[row].astype(f32)
        low = pltpu.roll(left[block], lax.rem(dil - 8 - 8 * j + 2 * side, side), 1)
        high = pltpu.roll(right[block], lax.rem(2 * side - dil - 8 * j, side), 1)
        before = jnp.where(lane < dil, low, pltpu.roll(x, dil, 1))
        after = jnp.where(lane >= side - dil, high, pltpu.roll(x, side - dil, 1))
        out_ref[row] = jnp.concatenate(
            [before.astype(bf16), centre[row], after.astype(bf16)], axis=0
        )
        return carry

    lax.fori_loop(0, height, body, 0, unroll=4)


def taps_of(stack_ref, p, dil, group):
    return jnp.concatenate(
        [
            jnp.concatenate(
                [stack_ref[p + k + reach + u * dil] for k in range(group)], axis=1
            )
            for u in (-1, 0, 1)
        ],
        axis=0,
    )


def backward_kernel(
    meta, x_ref, top, bot, left, right, w_ref, out_ref, stack_ref, centre, low, high, *, length
):
    side = x_ref.shape[0]
    dil = meta[0]
    keep = [meta[k].astype(f32) for k in range(1, 5)]
    centre[pl.ds(reach, side)] = x_ref[...]
    centre[pl.ds(0, reach)] = (top[...].astype(f32) * keep[0]).astype(bf16)
    centre[pl.ds(reach + side, reach)] = (bot[...].astype(f32) * keep[1]).astype(bf16)
    blocks = left.shape[0]
    for k in range(blocks):
        edge = keep[0] if k == 0 else keep[1] if k == blocks - 1 else 1.0
        low[k] = left[k].astype(f32) * (keep[2] * edge)
        high[k] = right[k].astype(f32) * (keep[3] * edge)
    stack_shifts(centre, low, high, stack_ref, dil)

    def body(step, carry):
        p = 4 * step
        got = jnp.dot(w_ref[...], taps_of(stack_ref, p, dil, 4), preferred_element_type=f32)
        for k in range(4):
            out_ref[p + k] = got[:, side * k : side * (k + 1)] * (1.0 / length)
        return carry

    lax.fori_loop(0, side // 4, body, 0)


def moments(stat, count):
    mean = stat[:, 0:1] / count
    var = stat[:, 1:2] / count - mean * mean
    return mean, lax.rsqrt(var + eps)


def forward_kernel(
    meta, ids, x_ref, top, bot, left, right, stat, gain, bias, col_ids, w_ref,
    hid_ref, act_ref, slope_ref, sums_ref,
    centre_a, centre_s, low_a, high_a, low_s, high_s, *, count,
):
    side, chans = x_ref.shape[0], x_ref.shape[1]
    dil = meta[0]
    keep = [meta[k].astype(f32) for k in range(1, 5)]
    mean, scale = moments(stat[...], count)
    mean = jnp.broadcast_to(mean, (chans, side))
    scale = jnp.broadcast_to(scale, (chans, side))
    gained = jnp.broadcast_to(gain[...], (chans, side))

    def activate(x):
        norm = (x.astype(f32) - mean) * scale
        z = gained * norm
        e = jnp.exp(jnp.minimum(z, 0.0))
        return jnp.where(z > 0, z, e - 1.0), jnp.where(z > 0, 1.0, e) * norm

    def inner(p, carry):
        a, s = activate(x_ref[p])
        centre_a[p + reach] = a.astype(bf16)
        centre_s[p + reach] = s.astype(bf16)
        return carry

    lax.fori_loop(0, side, inner, 0, unroll=4)
    for k in range(reach):
        a, s = activate(top[k])
        centre_a[k] = (a * keep[0]).astype(bf16)
        centre_s[k] = (s * keep[0]).astype(bf16)
        a, s = activate(bot[k])
        centre_a[reach + side + k] = (a * keep[1]).astype(bf16)
        centre_s[reach + side + k] = (s * keep[1]).astype(bf16)
    blocks = left.shape[0]
    for k in range(blocks):
        edge = keep[0] if k == 0 else keep[1] if k == blocks - 1 else 1.0
        a, s = activate(left[k])
        low_a[k] = a * (keep[2] * edge)
        low_s[k] = s * (keep[2] * edge)
        a, s = activate(right[k])
        high_a[k] = a * (keep[3] * edge)
        high_s[k] = s * (keep[3] * edge)
    stack_shifts(centre_a, low_a, high_a, act_ref, dil)
    stack_shifts(centre_s, low_s, high_s, slope_ref, dil)
    biased = jnp.broadcast_to(bias[...], (chans, side))
    cols = jnp.broadcast_to(col_ids[...], (chans, side))

    def body(step, carry):
        one, two = carry
        p = 4 * step
        got = jnp.dot(w_ref[...], taps_of(act_ref, p, dil, 4), preferred_element_type=f32)
        for k in range(4):
            hid = got[:, side * k : side * (k + 1)] + jnp.where(cols != ids[p + k], biased, 0.0)
            hid_ref[p + k] = hid
            one = one + hid
            two = two + hid * hid
        return one, two

    zero = jnp.zeros((chans, side), f32)
    sums_ref[...] = as_columns(lax.fori_loop(0, side // 4, body, (zero, zero)), chans, side)


def second_kernel(
    meta, hid_ref, dact_ref, stat, gain, stack_ref, sums_ref, grad_ref, act_ref, *, count
):
    side, chans = hid_ref.shape[0], hid_ref.shape[1]
    dil = meta[0]
    mean, scale = moments(stat[...], count)
    mean = jnp.broadcast_to(mean, (chans, side))
    scale = jnp.broadcast_to(scale, (chans, side))
    gained = jnp.broadcast_to(gain[...], (chans, side))
    grad_ref[...] = jnp.zeros_like(grad_ref)

    def body(step, carry):
        sums = list(carry)
        p = 4 * step
        acts = []
        for k in range(4):
            dact = dact_ref[p + k]
            norm = (hid_ref[p + k] - mean) * scale
            z = gained * norm
            e = jnp.exp(jnp.minimum(z, 0.0))
            act = jnp.where(z > 0, z, e - 1.0).astype(bf16)
            acts.append(act)
            dz = dact * jnp.where(z > 0, 1.0, e)
            dn = gained * dz
            sums[0] = sums[0] + dn
            sums[1] = sums[1] + dn * norm
            sums[2] = sums[2] + dz * norm
            sums[3] = sums[3] + act.astype(f32) * dact
        grad_ref[...] += lax.dot_general(
            taps_of(stack_ref, p, dil, 4),
            jnp.concatenate(acts, axis=1),
            (((1,), (1,)), ((), ())),
            preferred_element_type=f32,
        )
        return tuple(sums)

    zero = jnp.zeros((chans, side), f32)
    sums = lax.fori_loop(0, side // 4, body, (zero,) * 4)
    sums_ref[...] = as_columns(sums, chans, side)


def first_kernel(
    meta, ids, hid_ref, dact_ref, stat, stat_two, gain, col_ids, act_ref, slope_ref, w_ref,
    sums_ref, grad_ref, slope_grad, *, count,
):
    side, chans = hid_ref.shape[0], hid_ref.shape[1]
    dil = meta[0]
    mean, scale = moments(stat[...], count)
    mean = jnp.broadcast_to(mean, (chans, side))
    scale = jnp.broadcast_to(scale, (chans, side))
    gained = jnp.broadcast_to(gain[...], (chans, side))
    mean_a = jnp.broadcast_to(stat_two[:, 0:1] / count, (chans, side))
    mean_b = jnp.broadcast_to(stat_two[:, 1:2] / count, (chans, side))
    cols = jnp.broadcast_to(col_ids[...], (chans, side))
    grad_ref[...] = jnp.zeros_like(grad_ref)
    slope_grad[...] = jnp.zeros_like(slope_grad)

    def body(step, total):
        p = 4 * step
        lows = []
        for k in range(4):
            norm = (hid_ref[p + k] - mean) * scale
            z = gained * norm
            slope = jnp.where(z > 0, 1.0, jnp.exp(jnp.minimum(z, 0.0)))
            dn = gained * (dact_ref[p + k] * slope)
            dhid = (dn - mean_a - norm * mean_b) * scale
            total = total + jnp.where(cols != ids[p + k], dhid, 0.0)
            lows.append(dhid.astype(bf16))
        low = jnp.concatenate(lows, axis=1)
        dims = (((1,), (1,)), ((), ()))
        grad_ref[...] += lax.dot_general(
            taps_of(act_ref, p, dil, 4), low, dims, preferred_element_type=f32
        )
        slope_grad[...] += lax.dot_general(
            taps_of(slope_ref, p, dil, 4), low, dims, preferred_element_type=f32
        )
        return total

    total = lax.fori_loop(0, side // 4, body, jnp.zeros((chans, side), f32))
    gain_grad = jnp.zeros((chans, chans), f32)
    for t in range(9):
        part = pl.ds(t * chans, chans)
        gain_grad = gain_grad + slope_grad[part, :] * w_ref[part, :]
    lane = lanes(chans, side)
    sums_ref[...] = jnp.where(
        lane == 1, jnp.sum(gain_grad, axis=1, keepdims=True), as_columns([total], chans, side)
    )


def compute(kernel, name, outs, specs, scratch=()):
    return pl.pallas_call(
        kernel,
        name=name,
        out_shape=outs,
        in_specs=specs,
        out_specs=jax.tree.map(lambda _: vmem, outs),
        scratch_shapes=list(scratch),
        compiler_params=pltpu.CompilerParams(vmem_limit_bytes=LIMIT),
    )


def local(pair, cotangent, chain, dilation, w_one, w_two, gain_one, gain_two, inter_bias):
    chans, side = pair.shape[1], pair.shape[2]
    rows, cols = lax.axis_size("row"), lax.axis_size("col")
    length = side * rows
    count = float(length * length)
    blocks = side // 16
    height = side + 2 * reach
    r, c = lax.axis_index("row"), lax.axis_index("col")

    turned = jnp.transpose(pair[0], (2, 0, 1))
    mirrored = lax.ppermute(
        turned,
        ("row", "col"),
        [(i * cols + j, j * cols + i) for i in range(rows) for j in range(cols)],
    )
    cot = jnp.transpose(cotangent[0], (1, 0, 2))
    tile = jnp.transpose(pair[0], (1, 0, 2))

    keep = jnp.stack([r > 0, r < rows - 1, c > 0, c < cols - 1]).astype(jnp.int32)
    meta_one = jnp.concatenate([dilation[0:1], keep])
    meta_two = jnp.concatenate([dilation[1:2], keep])
    row_ids = lax.dynamic_slice_in_dim(chain[0], r * side, side)
    col_ids = lax.dynamic_slice_in_dim(chain[0], c * side, side)[None]
    gain_a, gain_b, bias = gain_one[:, None], gain_two[:, None], inter_bias[:, None]
    forward_w = jnp.transpose(w_one, (1, 0, 2)).reshape(chans, 9 * chans)
    backward_w = jnp.transpose(w_two[::-1], (2, 0, 1)).reshape(chans, 9 * chans)
    slope_w = jnp.transpose(w_one, (0, 2, 1)).reshape(9 * chans, chans).astype(f32)

    full = (side, chans, side)
    edge = shape((blocks, chans, side), bf16)
    stats = shape((chans, side), f32)
    stacked = shape((height, 3 * chans, side), bf16)
    centre = pltpu.VMEM((height, chans, side), bf16)
    border = pltpu.VMEM((blocks + 2, chans, side), f32)

    low, high = compute(edges_kernel, "edges", [edge, edge], [vmem])(cot)
    top, bot, left, right = halo(cot, low, high, 1)
    d_act, cot_stack = compute(
        functools.partial(backward_kernel, length=length),
        "backward",
        [shape(full, f32), stacked],
        [smem] + [vmem] * 6,
        [centre, border, border],
    )(meta_two, cot, top, bot, left, right, backward_w)

    sym, low, high, stat_one = compute(
        sym_kernel, "sym", [shape(full, bf16), edge, edge, stats], [vmem] * 3
    )(tile, mirrored, cot)
    top, bot, left, right = halo(sym, low, high, 2)
    all_one = all_stats(stat_one, 3)
    hid, act_stack, slope_stack, stat_two = compute(
        functools.partial(forward_kernel, count=count),
        "forward",
        [shape(full, f32), stacked, stacked, stats],
        [smem, smem] + [vmem] * 10,
        [centre, centre, border, border, border, border],
    )(meta_one, row_ids, sym, top, bot, left, right, all_one, gain_a, bias, col_ids, forward_w)
    all_two = all_stats(stat_two, 4)
    stat_three, grad_two = compute(
        functools.partial(second_kernel, count=count),
        "second",
        [stats, shape((9 * chans, chans), f32)],
        [smem] + [vmem] * 5,
        [pltpu.VMEM((8, 128), f32)],
    )(meta_two, hid, d_act, all_two, gain_b, cot_stack)
    all_three = all_stats(stat_three, 5)
    stat_four, grad_one = compute(
        functools.partial(first_kernel, count=count),
        "first",
        [stats, shape((9 * chans, chans), f32)],
        [smem, smem] + [vmem] * 9,
        [pltpu.VMEM((9 * chans, chans), f32)],
    )(
        meta_one, row_ids, hid, d_act, all_two, all_three, gain_b, col_ids, act_stack,
        slope_stack, slope_w,
    )

    loss = stat_one[:, 2] * (1.0 / length) + stat_three[:, 3]
    vectors = jnp.stack([stat_four[:, 1], stat_three[:, 2], stat_four[:, 0], loss])
    flat = jnp.concatenate(
        [grad_one.reshape(-1, 128), grad_two.reshape(-1, 128), vectors.reshape(-1, 128)]
    )
    total = grand_total(flat, 6)
    size = 9 * chans * chans // 128
    out_one = jnp.transpose(total[:size].reshape(9, chans, chans), (0, 2, 1))
    out_two = total[size : 2 * size].reshape(9, chans, chans)[::-1] * (1.0 / length)
    ends = total[2 * size :].reshape(4, chans)
    return out_one, out_two, ends[0], ends[1], ends[2], jnp.sum(ends[3])


def solution(mesh):
    in_specs = (
        P("dp", None, "row", "col"),
        P("dp", None, "row", "col"),
        P("dp", None),
        P(),
        P(),
        P(),
        P(),
        P(),
        P(),
    )
    out_specs = (P(), P(), P(), P(), P(), P())
    return jax.shard_map(local, mesh=mesh, in_specs=in_specs, out_specs=out_specs, check_vma=False)
```

```python
import functools

import jax
import jax.numpy as jnp
from jax import lax
from jax.experimental import pallas as pl
from jax.experimental.pallas import tpu as pltpu
from jax.sharding import PartitionSpec as P

reach = 8
eps = 1e-05
f32 = jnp.float32
bf16 = jnp.bfloat16
MESH = pl.DeviceIdType.MESH
vmem = pl.BlockSpec(memory_space=pltpu.VMEM)
smem = pl.BlockSpec(memory_space=pltpu.SMEM)
anyspace = pl.BlockSpec(memory_space=pl.ANY)
LIMIT = 56 * 1024 * 1024


def shape(dims, dtype):
    return jax.ShapeDtypeStruct(dims, dtype)


def lanes(chans=64, width=128):
    return lax.broadcasted_iota(jnp.int32, (chans, width), 1)


def pack_edges(rows, chans, side):
    group = lanes(chans, side) // reach
    low = jnp.zeros((chans, side), f32)
    high = jnp.zeros((chans, side), f32)
    for j, row in enumerate(rows):
        low = jnp.where(group == j, row if j == 0 else pltpu.roll(row, 8 * j, 1), low)
        shift = (8 * j + 8) % side
        high = jnp.where(group == j, row if shift == 0 else pltpu.roll(row, shift, 1), high)
    return low.astype(bf16), high.astype(bf16)


def as_columns(columns, chans, side):
    lane = lanes(chans, side)
    tile = jnp.zeros((chans, side), f32)
    for k, values in enumerate(columns):
        tile = jnp.where(lane == k, jnp.sum(values, axis=1, keepdims=True), tile)
    return tile


def edges_kernel(x_ref, low_ref, high_ref):
    side, chans = x_ref.shape[0], x_ref.shape[1]

    def body(k, carry):
        rows = [x_ref[16 * k + j].astype(f32) for j in range(16)]
        low_ref[k], high_ref[k] = pack_edges(rows, chans, side)
        return carry

    lax.fori_loop(0, side // 16, body, 0)


def sym_kernel(x_ref, first_ref, last_ref, cot_ref, sym_ref, low_ref, high_ref, stat_ref):
    side, chans = x_ref.shape[0], x_ref.shape[1]
    half = side // 2

    def body(m_ref, base, k, carry):
        one, two, three = carry
        rows = []
        for j in range(16):
            p = 16 * k + j
            sym = ((x_ref[p + base].astype(f32) + m_ref[p].astype(f32)) * 0.5).astype(bf16)
            sym_ref[p + base] = sym
            wide = sym.astype(f32)
            rows.append(wide)
            one = one + wide
            two = two + wide * wide
            three = three + wide * cot_ref[p + base].astype(f32)
        at = k + base // 16
        low_ref[at], high_ref[at] = pack_edges(rows, chans, side)
        return one, two, three

    zero = jnp.zeros((chans, side), f32)
    sums = (zero, zero, zero)
    for m_ref, base in ((first_ref, 0), (last_ref, half)):
        sums = lax.fori_loop(0, half // 16, functools.partial(body, m_ref, base), sums)
    stat_ref[...] = as_columns(sums, chans, side)


def halo_body(x_ref, low_ref, high_ref, top_ref, bot_ref, left_ref, right_ref, send, recv):
    rows, cols = lax.axis_size("row"), lax.axis_size("col")
    r, c = lax.axis_index("row"), lax.axis_index("col")
    up, down = lax.rem(r + rows - 1, rows), lax.rem(r + 1, rows)
    lef, rig = lax.rem(c + cols - 1, cols), lax.rem(c + 1, cols)
    side, blocks = x_ref.shape[0], low_ref.shape[0]
    moves = [
        (high_ref, left_ref.at[pl.ds(1, blocks)], r, rig),
        (low_ref, right_ref.at[pl.ds(1, blocks)], r, lef),
        (x_ref.at[pl.ds(side - reach, reach)], top_ref, down, c),
        (x_ref.at[pl.ds(0, reach)], bot_ref, up, c),
        (high_ref.at[pl.ds(blocks - 1, 1)], left_ref.at[pl.ds(0, 1)], down, rig),
        (high_ref.at[pl.ds(0, 1)], left_ref.at[pl.ds(blocks + 1, 1)], up, rig),
        (low_ref.at[pl.ds(blocks - 1, 1)], right_ref.at[pl.ds(0, 1)], down, lef),
        (low_ref.at[pl.ds(0, 1)], right_ref.at[pl.ds(blocks + 1, 1)], up, lef),
    ]
    return [
        pltpu.make_async_remote_copy(
            src_ref=src,
            dst_ref=dst,
            send_sem=send.at[n],
            recv_sem=recv.at[n],
            device_id={"row": to_row, "col": to_col},
            device_id_type=MESH,
        )
        for n, (src, dst, to_row, to_col) in enumerate(moves)
    ]


def halo_kernel(x_ref, low_ref, high_ref, top_ref, bot_ref, left_ref, right_ref, send, recv):
    rows, cols = lax.axis_size("row"), lax.axis_size("col")
    r, c = lax.axis_index("row"), lax.axis_index("col")
    barrier = pltpu.get_barrier_semaphore()
    for a in (-1, 0, 1):
        for b in (-1, 0, 1):
            if a or b:
                pl.semaphore_signal(
                    barrier,
                    inc=1,
                    device_id={
                        "row": lax.rem(r + rows + a, rows),
                        "col": lax.rem(c + cols + b, cols),
                    },
                    device_id_type=MESH,
                )
    pl.semaphore_wait(barrier, 8)
    copies = halo_body(x_ref, low_ref, high_ref, top_ref, bot_ref, left_ref, right_ref, send, recv)
    for copy in copies:
        copy.start()
    for copy in copies:
        copy.wait()


def halo(x, low, high, number):
    side, chans, width = x.shape
    blocks = low.shape[0]
    return pl.pallas_call(
        halo_kernel,
        name="halo",
        out_shape=[
            shape((reach, chans, width), bf16),
            shape((reach, chans, width), bf16),
            shape((blocks + 2, chans, width), bf16),
            shape((blocks + 2, chans, width), bf16),
        ],
        in_specs=[anyspace] * 3,
        out_specs=[anyspace] * 4,
        scratch_shapes=[pltpu.SemaphoreType.DMA((8,)), pltpu.SemaphoreType.DMA((8,))],
        compiler_params=pltpu.CompilerParams(collective_id=number, has_side_effects=True),
    )(x, low, high)


def peer_of(index, cols, depth):
    return {
        "row": index // (cols * depth),
        "col": lax.rem(index // depth, cols),
        "dp": lax.rem(index, depth),
    }


def greet(barrier, me, count, peer):
    def body(step, carry):
        to = lax.rem(me + step, count)
        pl.semaphore_signal(barrier, inc=1, device_id=peer(to), device_id_type=MESH)
        return carry

    lax.fori_loop(1, count, body, 0)
    pl.semaphore_wait(barrier, count - 1)


def stats_kernel(x_ref, out_ref, own, slots, send, recv):
    rows, cols = lax.axis_size("row"), lax.axis_size("col")
    count = rows * cols
    me = lax.axis_index("row") * cols + lax.axis_index("col")
    chans = x_ref.shape[0]

    def peer(index):
        return {"row": index // cols, "col": lax.rem(index, cols)}

    greet(pltpu.get_barrier_semaphore(), me, count, peer)
    own[...] = x_ref[...].T[0:8, :]

    def copy_to(step):
        return pltpu.make_async_remote_copy(
            src_ref=own,
            dst_ref=slots.at[me],
            send_sem=send.at[step],
            recv_sem=recv.at[me],
            device_id=peer(lax.rem(me + step, count)),
            device_id_type=MESH,
        )

    def copy_from(step):
        source = lax.rem(me + step, count)
        return pltpu.make_async_remote_copy(
            src_ref=own,
            dst_ref=slots.at[source],
            send_sem=send.at[step],
            recv_sem=recv.at[source],
            device_id=peer(source),
            device_id_type=MESH,
        )

    def start(step, carry):
        copy_to(step).start()
        return carry

    def land(step, carry):
        copy_to(step).wait_send()
        copy_from(step).wait_recv()
        return carry

    slots[me] = own[...]
    lax.fori_loop(1, count, start, 0)
    lax.fori_loop(1, count, land, 0)
    total = jnp.sum(slots[...], axis=0)
    filled = jnp.concatenate([total, jnp.zeros((x_ref.shape[1] - 8, chans), f32)], axis=0)
    out_ref[...] = filled.T


def all_stats(tile, number):
    count = lax.axis_size("row") * lax.axis_size("col")
    chans = tile.shape[0]
    return pl.pallas_call(
        stats_kernel,
        name="stats",
        out_shape=shape(tile.shape, f32),
        in_specs=[vmem],
        out_specs=vmem,
        scratch_shapes=[
            pltpu.VMEM((8, chans), f32),
            pltpu.VMEM((count, 8, chans), f32),
            pltpu.SemaphoreType.DMA((count,)),
            pltpu.SemaphoreType.DMA((count,)),
        ],
        compiler_params=pltpu.CompilerParams(collective_id=number, has_side_effects=True),
    )(tile)


def total_kernel(x_ref, out_ref, slots, send, recv, send_two, recv_two):
    rows, cols, depth = lax.axis_size("row"), lax.axis_size("col"), lax.axis_size("dp")
    count = rows * cols * depth
    me = (lax.axis_index("row") * cols + lax.axis_index("col")) * depth + lax.axis_index("dp")
    peer = functools.partial(peer_of, cols=cols, depth=depth)
    greet(pltpu.get_barrier_semaphore(), me, count, peer)

    def scatter(step, source):
        to = lax.rem(me + step, count)
        return pltpu.make_async_remote_copy(
            src_ref=x_ref.at[to],
            dst_ref=slots.at[source],
            send_sem=send.at[step],
            recv_sem=recv.at[source],
            device_id=peer(to),
            device_id_type=MESH,
        )

    def gather(step, source):
        to = lax.rem(me + step, count)
        return pltpu.make_async_remote_copy(
            src_ref=out_ref.at[source],
            dst_ref=out_ref.at[source],
            send_sem=send_two.at[step],
            recv_sem=recv_two.at[source],
            device_id=peer(to),
            device_id_type=MESH,
        )

    def run(make):
        def start(step, carry):
            make(step, me).start()
            return carry

        def land(step, carry):
            make(step, me).wait_send()
            make(step, lax.rem(me + step, count)).wait_recv()
            return carry

        lax.fori_loop(1, count, start, 0)
        lax.fori_loop(1, count, land, 0)

    slots[me] = x_ref[me]
    run(scatter)
    out_ref[me] = jnp.sum(slots[...], axis=0)
    run(gather)


def grand_total(flat, number):
    count = lax.axis_size("row") * lax.axis_size("col") * lax.axis_size("dp")
    rows = flat.shape[0]
    each = -(-rows // (8 * count)) * 8
    padded = jnp.pad(flat, ((0, each * count - rows), (0, 0))).reshape(count, each, 128)
    out = pl.pallas_call(
        total_kernel,
        name="total",
        out_shape=shape(padded.shape, f32),
        in_specs=[vmem],
        out_specs=vmem,
        scratch_shapes=[pltpu.VMEM(padded.shape, f32)] + [pltpu.SemaphoreType.DMA((count,))] * 4,
        compiler_params=pltpu.CompilerParams(
            collective_id=number, has_side_effects=True, vmem_limit_bytes=LIMIT
        ),
    )(padded)
    return out.reshape(each * count, 128)[:rows]


def stack_shifts(centre, left, right, out_ref, dil):
    height, chans, side = centre.shape
    lane = lanes(chans, side)

    def body(row, carry):
        block, j = (row + reach) // 16, lax.rem(row + reach, 16)
        x = centre[row].astype(f32)
        low = pltpu.roll(left[block], lax.rem(dil - 8 - 8 * j + 2 * side, side), 1)
        high = pltpu.roll(right[block], lax.rem(2 * side - dil - 8 * j, side), 1)
        before = jnp.where(lane < dil, low, pltpu.roll(x, dil, 1))
        after = jnp.where(lane >= side - dil, high, pltpu.roll(x, side - dil, 1))
        out_ref[row] = jnp.concatenate(
            [before.astype(bf16), centre[row], after.astype(bf16)], axis=0
        )
        return carry

    lax.fori_loop(0, height, body, 0, unroll=4)


def taps_of(stack_ref, p, dil, group):
    return jnp.concatenate(
        [
            jnp.concatenate(
                [stack_ref[p + k + reach + u * dil] for k in range(group)], axis=1
            )
            for u in (-1, 0, 1)
        ],
        axis=0,
    )


def backward_kernel(
    meta, x_ref, top, bot, left, right, w_ref, out_ref, stack_ref, centre, low, high, *, length
):
    side = x_ref.shape[0]
    dil = meta[0]
    keep = [meta[k].astype(f32) for k in range(1, 5)]
    centre[pl.ds(reach, side)] = x_ref[...]
    centre[pl.ds(0, reach)] = (top[...].astype(f32) * keep[0]).astype(bf16)
    centre[pl.ds(reach + side, reach)] = (bot[...].astype(f32) * keep[1]).astype(bf16)
    blocks = left.shape[0]
    for k in range(blocks):
        edge = keep[0] if k == 0 else keep[1] if k == blocks - 1 else 1.0
        low[k] = left[k].astype(f32) * (keep[2] * edge)
        high[k] = right[k].astype(f32) * (keep[3] * edge)
    stack_shifts(centre, low, high, stack_ref, dil)

    def body(step, carry):
        p = 4 * step
        got = jnp.dot(w_ref[...], taps_of(stack_ref, p, dil, 4), preferred_element_type=f32)
        for k in range(4):
            out_ref[p + k] = got[:, side * k : side * (k + 1)] * (1.0 / length)
        return carry

    lax.fori_loop(0, side // 4, body, 0)


def moments(stat, count):
    mean = stat[:, 0:1] / count
    var = stat[:, 1:2] / count - mean * mean
    return mean, lax.rsqrt(var + eps)


def forward_kernel(
    meta, ids, x_ref, top, bot, left, right, stat, gain, bias, col_ids, w_ref,
    hid_ref, act_ref, slope_ref, sums_ref,
    centre_a, centre_s, low_a, high_a, low_s, high_s, *, count,
):
    side, chans = x_ref.shape[0], x_ref.shape[1]
    dil = meta[0]
    keep = [meta[k].astype(f32) for k in range(1, 5)]
    mean, scale = moments(stat[...], count)
    mean = jnp.broadcast_to(mean, (chans, side))
    scale = jnp.broadcast_to(scale, (chans, side))
    gained = jnp.broadcast_to(gain[...], (chans, side))

    def activate(x):
        norm = (x.astype(f32) - mean) * scale
        z = gained * norm
        e = jnp.exp(jnp.minimum(z, 0.0))
        return jnp.where(z > 0, z, e - 1.0), jnp.where(z > 0, 1.0, e) * norm

    def inner(p, carry):
        a, s = activate(x_ref[p])
        centre_a[p + reach] = a.astype(bf16)
        centre_s[p + reach] = s.astype(bf16)
        return carry

    lax.fori_loop(0, side, inner, 0, unroll=4)
    for k in range(reach):
        a, s = activate(top[k])
        centre_a[k] = (a * keep[0]).astype(bf16)
        centre_s[k] = (s * keep[0]).astype(bf16)
        a, s = activate(bot[k])
        centre_a[reach + side + k] = (a * keep[1]).astype(bf16)
        centre_s[reach + side + k] = (s * keep[1]).astype(bf16)
    blocks = left.shape[0]
    for k in range(blocks):
        edge = keep[0] if k == 0 else keep[1] if k == blocks - 1 else 1.0
        a, s = activate(left[k])
        low_a[k] = a * (keep[2] * edge)
        low_s[k] = s * (keep[2] * edge)
        a, s = activate(right[k])
        high_a[k] = a * (keep[3] * edge)
        high_s[k] = s * (keep[3] * edge)
    stack_shifts(centre_a, low_a, high_a, act_ref, dil)
    stack_shifts(centre_s, low_s, high_s, slope_ref, dil)
    biased = jnp.broadcast_to(bias[...], (chans, side))
    cols = jnp.broadcast_to(col_ids[...], (chans, side))

    def body(step, carry):
        one, two = carry
        p = 4 * step
        got = jnp.dot(w_ref[...], taps_of(act_ref, p, dil, 4), preferred_element_type=f32)
        for k in range(4):
            hid = got[:, side * k : side * (k + 1)] + jnp.where(cols != ids[p + k], biased, 0.0)
            hid_ref[p + k] = hid
            one = one + hid
            two = two + hid * hid
        return one, two

    zero = jnp.zeros((chans, side), f32)
    sums_ref[...] = as_columns(lax.fori_loop(0, side // 4, body, (zero, zero)), chans, side)


def second_kernel(
    meta, hid_ref, dact_ref, stat, gain, stack_ref, sums_ref, grad_ref, act_ref, *, count
):
    side, chans = hid_ref.shape[0], hid_ref.shape[1]
    dil = meta[0]
    mean, scale = moments(stat[...], count)
    mean = jnp.broadcast_to(mean, (chans, side))
    scale = jnp.broadcast_to(scale, (chans, side))
    gained = jnp.broadcast_to(gain[...], (chans, side))
    grad_ref[...] = jnp.zeros_like(grad_ref)

    def body(step, carry):
        sums = list(carry)
        p = 4 * step
        acts = []
        for k in range(4):
            dact = dact_ref[p + k]
            norm = (hid_ref[p + k] - mean) * scale
            z = gained * norm
            e = jnp.exp(jnp.minimum(z, 0.0))
            act = jnp.where(z > 0, z, e - 1.0).astype(bf16)
            acts.append(act)
            dz = dact * jnp.where(z > 0, 1.0, e)
            dn = gained * dz
            sums[0] = sums[0] + dn
            sums[1] = sums[1] + dn * norm
            sums[2] = sums[2] + dz * norm
            sums[3] = sums[3] + act.astype(f32) * dact
        grad_ref[...] += lax.dot_general(
            taps_of(stack_ref, p, dil, 4),
            jnp.concatenate(acts, axis=1),
            (((1,), (1,)), ((), ())),
            preferred_element_type=f32,
        )
        return tuple(sums)

    zero = jnp.zeros((chans, side), f32)
    sums = lax.fori_loop(0, side // 4, body, (zero,) * 4)
    sums_ref[...] = as_columns(sums, chans, side)


def first_kernel(
    meta, ids, hid_ref, dact_ref, stat, stat_two, gain, col_ids, act_ref, slope_ref, w_ref,
    sums_ref, grad_ref, slope_grad, *, count,
):
    side, chans = hid_ref.shape[0], hid_ref.shape[1]
    dil = meta[0]
    mean, scale = moments(stat[...], count)
    mean = jnp.broadcast_to(mean, (chans, side))
    scale = jnp.broadcast_to(scale, (chans, side))
    gained = jnp.broadcast_to(gain[...], (chans, side))
    mean_a = jnp.broadcast_to(stat_two[:, 0:1] / count, (chans, side))
    mean_b = jnp.broadcast_to(stat_two[:, 1:2] / count, (chans, side))
    cols = jnp.broadcast_to(col_ids[...], (chans, side))
    grad_ref[...] = jnp.zeros_like(grad_ref)
    slope_grad[...] = jnp.zeros_like(slope_grad)

    def body(step, total):
        p = 4 * step
        lows = []
        for k in range(4):
            norm = (hid_ref[p + k] - mean) * scale
            z = gained * norm
            slope = jnp.where(z > 0, 1.0, jnp.exp(jnp.minimum(z, 0.0)))
            dn = gained * (dact_ref[p + k] * slope)
            dhid = (dn - mean_a - norm * mean_b) * scale
            total = total + jnp.where(cols != ids[p + k], dhid, 0.0)
            lows.append(dhid.astype(bf16))
        low = jnp.concatenate(lows, axis=1)
        dims = (((1,), (1,)), ((), ()))
        grad_ref[...] += lax.dot_general(
            taps_of(act_ref, p, dil, 4), low, dims, preferred_element_type=f32
        )
        slope_grad[...] += lax.dot_general(
            taps_of(slope_ref, p, dil, 4), low, dims, preferred_element_type=f32
        )
        return total

    total = lax.fori_loop(0, side // 4, body, jnp.zeros((chans, side), f32))
    gain_grad = jnp.zeros((chans, chans), f32)
    for t in range(9):
        part = pl.ds(t * chans, chans)
        gain_grad = gain_grad + slope_grad[part, :] * w_ref[part, :]
    lane = lanes(chans, side)
    sums_ref[...] = jnp.where(
        lane == 1, jnp.sum(gain_grad, axis=1, keepdims=True), as_columns([total], chans, side)
    )


def compute(kernel, name, outs, specs, scratch=()):
    return pl.pallas_call(
        kernel,
        name=name,
        out_shape=outs,
        in_specs=specs,
        out_specs=jax.tree.map(lambda _: vmem, outs),
        scratch_shapes=list(scratch),
        compiler_params=pltpu.CompilerParams(vmem_limit_bytes=LIMIT),
    )


def local(pair, cotangent, chain, dilation, w_one, w_two, gain_one, gain_two, inter_bias):
    chans, side = pair.shape[1], pair.shape[2]
    rows, cols = lax.axis_size("row"), lax.axis_size("col")
    length = side * rows
    count = float(length * length)
    blocks = side // 16
    height = side + 2 * reach
    r, c = lax.axis_index("row"), lax.axis_index("col")

    cot = jnp.transpose(cotangent[0], (1, 0, 2))
    tile = jnp.transpose(pair[0], (1, 0, 2))

    keep = jnp.stack([r > 0, r < rows - 1, c > 0, c < cols - 1]).astype(jnp.int32)
    meta_one = jnp.concatenate([dilation[0:1], keep])
    meta_two = jnp.concatenate([dilation[1:2], keep])
    row_ids = lax.dynamic_slice_in_dim(chain[0], r * side, side)
    col_ids = lax.dynamic_slice_in_dim(chain[0], c * side, side)[None]
    gain_a, gain_b, bias = gain_one[:, None], gain_two[:, None], inter_bias[:, None]
    forward_w = jnp.transpose(w_one, (1, 0, 2)).reshape(chans, 9 * chans)
    backward_w = jnp.transpose(w_two[::-1], (2, 0, 1)).reshape(chans, 9 * chans)
    slope_w = jnp.transpose(w_one, (0, 2, 1)).reshape(9 * chans, chans).astype(f32)

    full = (side, chans, side)
    edge = shape((blocks, chans, side), bf16)
    stats = shape((chans, side), f32)
    stacked = shape((height, 3 * chans, side), bf16)
    centre = pltpu.VMEM((height, chans, side), bf16)
    border = pltpu.VMEM((blocks + 2, chans, side), f32)

    low, high = compute(edges_kernel, "edges", [edge, edge], [vmem])(cot)
    top, bot, left, right = halo(cot, low, high, 1)
    source, top = lax.optimization_barrier((pair[0], top))
    turned = jnp.transpose(source, (2, 0, 1))
    flip = 2 if rows % 4 == 0 else 1
    pairs = [(i, j) for i in range(rows) for j in range(cols)]
    aside = lax.ppermute(
        turned[side // 2 :],
        ("row", "col"),
        [(i * cols + j, (i ^ flip) * cols + j) for i, j in pairs],
    )
    direct = lax.ppermute(
        turned[: side // 2], ("row", "col"), [(i * cols + j, j * cols + i) for i, j in pairs]
    )
    onward = lax.ppermute(
        aside, ("row", "col"), [((i ^ flip) * cols + j, j * cols + i) for i, j in pairs]
    )
    d_act, cot_stack = compute(
        functools.partial(backward_kernel, length=length),
        "backward",
        [shape(full, f32), stacked],
        [smem] + [vmem] * 6,
        [centre, border, border],
    )(meta_two, cot, top, bot, left, right, backward_w)

    sym, low, high, stat_one = compute(
        sym_kernel, "sym", [shape(full, bf16), edge, edge, stats], [vmem] * 4
    )(tile, direct, onward, cot)
    top, bot, left, right = halo(sym, low, high, 2)
    all_one = all_stats(stat_one, 3)
    hid, act_stack, slope_stack, stat_two = compute(
        functools.partial(forward_kernel, count=count),
        "forward",
        [shape(full, f32), stacked, stacked, stats],
        [smem, smem] + [vmem] * 10,
        [centre, centre, border, border, border, border],
    )(meta_one, row_ids, sym, top, bot, left, right, all_one, gain_a, bias, col_ids, forward_w)
    all_two = all_stats(stat_two, 4)
    stat_three, grad_two = compute(
        functools.partial(second_kernel, count=count),
        "second",
        [stats, shape((9 * chans, chans), f32)],
        [smem] + [vmem] * 5,
        [pltpu.VMEM((8, 128), f32)],
    )(meta_two, hid, d_act, all_two, gain_b, cot_stack)
    all_three = all_stats(stat_three, 5)
    stat_four, grad_one = compute(
        functools.partial(first_kernel, count=count),
        "first",
        [stats, shape((9 * chans, chans), f32)],
        [smem, smem] + [vmem] * 9,
        [pltpu.VMEM((9 * chans, chans), f32)],
    )(
        meta_one, row_ids, hid, d_act, all_two, all_three, gain_b, col_ids, act_stack,
        slope_stack, slope_w,
    )

    loss = stat_one[:, 2] * (1.0 / length) + stat_three[:, 3]
    vectors = jnp.stack([stat_four[:, 1], stat_three[:, 2], stat_four[:, 0], loss])
    flat = jnp.concatenate(
        [grad_one.reshape(-1, 128), grad_two.reshape(-1, 128), vectors.reshape(-1, 128)]
    )
    total = grand_total(flat, 6)
    size = 9 * chans * chans // 128
    out_one = jnp.transpose(total[:size].reshape(9, chans, chans), (0, 2, 1))
    out_two = total[size : 2 * size].reshape(9, chans, chans)[::-1] * (1.0 / length)
    ends = total[2 * size :].reshape(4, chans)
    return out_one, out_two, ends[0], ends[1], ends[2], jnp.sum(ends[3])


def solution(mesh):
    in_specs = (
        P("dp", None, "row", "col"),
        P("dp", None, "row", "col"),
        P("dp", None),
        P(),
        P(),
        P(),
        P(),
        P(),
        P(),
    )
    out_specs = (P(), P(), P(), P(), P(), P())
    return jax.shard_map(local, mesh=mesh, in_specs=in_specs, out_specs=out_specs, check_vma=False)
```

```python
import functools

import jax
import jax.numpy as jnp
from jax import lax
from jax.experimental import pallas as pl
from jax.experimental.pallas import tpu as pltpu
from jax.sharding import PartitionSpec as P

reach = 8
eps = 1e-05
f32 = jnp.float32
bf16 = jnp.bfloat16
MESH = pl.DeviceIdType.MESH
vmem = pl.BlockSpec(memory_space=pltpu.VMEM)
smem = pl.BlockSpec(memory_space=pltpu.SMEM)
anyspace = pl.BlockSpec(memory_space=pl.ANY)
LIMIT = 56 * 1024 * 1024


def shape(dims, dtype):
    return jax.ShapeDtypeStruct(dims, dtype)


def lanes(chans=64, width=128):
    return lax.broadcasted_iota(jnp.int32, (chans, width), 1)


def pack_edges(rows, chans, side):
    group = lanes(chans, side) // reach
    low = jnp.zeros((chans, side), f32)
    high = jnp.zeros((chans, side), f32)
    for j, row in enumerate(rows):
        low = jnp.where(group == j, row if j == 0 else pltpu.roll(row, 8 * j, 1), low)
        shift = (8 * j + 8) % side
        high = jnp.where(group == j, row if shift == 0 else pltpu.roll(row, shift, 1), high)
    return low.astype(bf16), high.astype(bf16)


def as_columns(columns, chans, side):
    lane = lanes(chans, side)
    tile = jnp.zeros((chans, side), f32)
    for k, values in enumerate(columns):
        tile = jnp.where(lane == k, jnp.sum(values, axis=1, keepdims=True), tile)
    return tile


def edges_kernel(x_ref, low_ref, high_ref):
    side, chans = x_ref.shape[0], x_ref.shape[1]

    def body(k, carry):
        rows = [x_ref[16 * k + j].astype(f32) for j in range(16)]
        low_ref[k], high_ref[k] = pack_edges(rows, chans, side)
        return carry

    lax.fori_loop(0, side // 16, body, 0)


def sym_kernel(x_ref, first_ref, last_ref, cot_ref, sym_ref, low_ref, high_ref, stat_ref):
    side, chans = x_ref.shape[0], x_ref.shape[1]
    half = side // 2

    def body(m_ref, base, k, carry):
        one, two, three = carry
        rows = []
        for j in range(16):
            p = 16 * k + j
            sym = ((x_ref[p + base].astype(f32) + m_ref[p].astype(f32)) * 0.5).astype(bf16)
            sym_ref[p + base] = sym
            wide = sym.astype(f32)
            rows.append(wide)
            one = one + wide
            two = two + wide * wide
            three = three + wide * cot_ref[p + base].astype(f32)
        at = k + base // 16
        low_ref[at], high_ref[at] = pack_edges(rows, chans, side)
        return one, two, three

    zero = jnp.zeros((chans, side), f32)
    sums = (zero, zero, zero)
    for m_ref, base in ((first_ref, 0), (last_ref, half)):
        sums = lax.fori_loop(0, half // 16, functools.partial(body, m_ref, base), sums)
    stat_ref[...] = as_columns(sums, chans, side)


def halo_body(x_ref, low_ref, high_ref, top_ref, bot_ref, left_ref, right_ref, send, recv):
    rows, cols = lax.axis_size("row"), lax.axis_size("col")
    r, c = lax.axis_index("row"), lax.axis_index("col")
    up, down = lax.rem(r + rows - 1, rows), lax.rem(r + 1, rows)
    lef, rig = lax.rem(c + cols - 1, cols), lax.rem(c + 1, cols)
    side, blocks = x_ref.shape[0], low_ref.shape[0]
    moves = [
        (high_ref, left_ref.at[pl.ds(1, blocks)], r, rig),
        (low_ref, right_ref.at[pl.ds(1, blocks)], r, lef),
        (x_ref.at[pl.ds(side - reach, reach)], top_ref, down, c),
        (x_ref.at[pl.ds(0, reach)], bot_ref, up, c),
        (high_ref.at[pl.ds(blocks - 1, 1)], left_ref.at[pl.ds(0, 1)], down, rig),
        (high_ref.at[pl.ds(0, 1)], left_ref.at[pl.ds(blocks + 1, 1)], up, rig),
        (low_ref.at[pl.ds(blocks - 1, 1)], right_ref.at[pl.ds(0, 1)], down, lef),
        (low_ref.at[pl.ds(0, 1)], right_ref.at[pl.ds(blocks + 1, 1)], up, lef),
    ]
    return [
        pltpu.make_async_remote_copy(
            src_ref=src,
            dst_ref=dst,
            send_sem=send.at[n],
            recv_sem=recv.at[n],
            device_id={"row": to_row, "col": to_col},
            device_id_type=MESH,
        )
        for n, (src, dst, to_row, to_col) in enumerate(moves)
    ]


def halo_kernel(x_ref, low_ref, high_ref, top_ref, bot_ref, left_ref, right_ref, send, recv):
    rows, cols = lax.axis_size("row"), lax.axis_size("col")
    r, c = lax.axis_index("row"), lax.axis_index("col")
    barrier = pltpu.get_barrier_semaphore()
    for a in (-1, 0, 1):
        for b in (-1, 0, 1):
            if a or b:
                pl.semaphore_signal(
                    barrier,
                    inc=1,
                    device_id={
                        "row": lax.rem(r + rows + a, rows),
                        "col": lax.rem(c + cols + b, cols),
                    },
                    device_id_type=MESH,
                )
    pl.semaphore_wait(barrier, 8)
    copies = halo_body(x_ref, low_ref, high_ref, top_ref, bot_ref, left_ref, right_ref, send, recv)
    for copy in copies:
        copy.start()
    for copy in copies:
        copy.wait()


def halo(x, low, high, number):
    side, chans, width = x.shape
    blocks = low.shape[0]
    return pl.pallas_call(
        halo_kernel,
        name="halo",
        out_shape=[
            shape((reach, chans, width), bf16),
            shape((reach, chans, width), bf16),
            shape((blocks + 2, chans, width), bf16),
            shape((blocks + 2, chans, width), bf16),
        ],
        in_specs=[anyspace] * 3,
        out_specs=[anyspace] * 4,
        scratch_shapes=[pltpu.SemaphoreType.DMA((8,)), pltpu.SemaphoreType.DMA((8,))],
        compiler_params=pltpu.CompilerParams(collective_id=number, has_side_effects=True),
    )(x, low, high)


def greet(barrier, me, count, peer):
    def body(step, carry):
        to = lax.rem(me + step, count)
        pl.semaphore_signal(barrier, inc=1, device_id=peer(to), device_id_type=MESH)
        return carry

    lax.fori_loop(1, count, body, 0)
    pl.semaphore_wait(barrier, count - 1)


def stats_kernel(x_ref, out_ref, own, slots, send, recv):
    rows, cols = lax.axis_size("row"), lax.axis_size("col")
    count = rows * cols
    me = lax.axis_index("row") * cols + lax.axis_index("col")
    chans = x_ref.shape[0]

    def peer(index):
        return {"row": index // cols, "col": lax.rem(index, cols)}

    greet(pltpu.get_barrier_semaphore(), me, count, peer)
    own[...] = x_ref[...].T[0:8, :]

    def copy_to(step):
        return pltpu.make_async_remote_copy(
            src_ref=own,
            dst_ref=slots.at[me],
            send_sem=send.at[step],
            recv_sem=recv.at[me],
            device_id=peer(lax.rem(me + step, count)),
            device_id_type=MESH,
        )

    def copy_from(step):
        source = lax.rem(me + step, count)
        return pltpu.make_async_remote_copy(
            src_ref=own,
            dst_ref=slots.at[source],
            send_sem=send.at[step],
            recv_sem=recv.at[source],
            device_id=peer(source),
            device_id_type=MESH,
        )

    def start(step, carry):
        copy_to(step).start()
        return carry

    def land(step, carry):
        copy_to(step).wait_send()
        copy_from(step).wait_recv()
        return carry

    slots[me] = own[...]
    lax.fori_loop(1, count, start, 0)
    lax.fori_loop(1, count, land, 0)
    total = jnp.sum(slots[...], axis=0)
    filled = jnp.concatenate([total, jnp.zeros((x_ref.shape[1] - 8, chans), f32)], axis=0)
    out_ref[...] = filled.T


def border_stats_kernel(
    tile_ref, x_ref, low_ref, high_ref, out_ref, top_ref, bot_ref, left_ref, right_ref,
    own, slots, send, recv, halo_send, halo_recv,
):
    rows, cols = lax.axis_size("row"), lax.axis_size("col")
    count = rows * cols
    me = lax.axis_index("row") * cols + lax.axis_index("col")
    chans = tile_ref.shape[0]

    def peer(index):
        return {"row": index // cols, "col": lax.rem(index, cols)}

    greet(pltpu.get_barrier_semaphore(), me, count, peer)
    copies = halo_body(
        x_ref, low_ref, high_ref, top_ref, bot_ref, left_ref, right_ref, halo_send, halo_recv
    )
    for copy in copies:
        copy.start()
    own[...] = tile_ref[...].T[0:8, :]

    def copy_of(step, slot):
        return pltpu.make_async_remote_copy(
            src_ref=own,
            dst_ref=slots.at[slot],
            send_sem=send.at[step],
            recv_sem=recv.at[slot],
            device_id=peer(lax.rem(me + step, count)),
            device_id_type=MESH,
        )

    def start(step, carry):
        copy_of(step, me).start()
        return carry

    def land(step, carry):
        copy_of(step, me).wait_send()
        copy_of(step, lax.rem(me + step, count)).wait_recv()
        return carry

    slots[me] = own[...]
    lax.fori_loop(1, count, start, 0)
    lax.fori_loop(1, count, land, 0)
    total = jnp.sum(slots[...], axis=0)
    filled = jnp.concatenate([total, jnp.zeros((tile_ref.shape[1] - 8, chans), f32)], axis=0)
    out_ref[...] = filled.T
    for copy in copies:
        copy.wait()


def border_stats(tile, x, low, high, number):
    side, chans, width = x.shape
    blocks = low.shape[0]
    count = lax.axis_size("row") * lax.axis_size("col")
    return pl.pallas_call(
        border_stats_kernel,
        name="border_stats",
        out_shape=[
            shape(tile.shape, f32),
            shape((reach, chans, width), bf16),
            shape((reach, chans, width), bf16),
            shape((blocks + 2, chans, width), bf16),
            shape((blocks + 2, chans, width), bf16),
        ],
        in_specs=[vmem] + [anyspace] * 3,
        out_specs=[vmem] + [anyspace] * 4,
        scratch_shapes=[
            pltpu.VMEM((8, chans), f32),
            pltpu.VMEM((count, 8, chans), f32),
            pltpu.SemaphoreType.DMA((count,)),
            pltpu.SemaphoreType.DMA((count,)),
            pltpu.SemaphoreType.DMA((8,)),
            pltpu.SemaphoreType.DMA((8,)),
        ],
        compiler_params=pltpu.CompilerParams(collective_id=number, has_side_effects=True),
    )(tile, x, low, high)


def all_stats(tile, number):
    count = lax.axis_size("row") * lax.axis_size("col")
    chans = tile.shape[0]
    return pl.pallas_call(
        stats_kernel,
        name="stats",
        out_shape=shape(tile.shape, f32),
        in_specs=[vmem],
        out_specs=vmem,
        scratch_shapes=[
            pltpu.VMEM((8, chans), f32),
            pltpu.VMEM((count, 8, chans), f32),
            pltpu.SemaphoreType.DMA((count,)),
            pltpu.SemaphoreType.DMA((count,)),
        ],
        compiler_params=pltpu.CompilerParams(collective_id=number, has_side_effects=True),
    )(tile)


def total_kernel(x_ref, out_ref, slots, part, col_slots, *sems):
    rows, cols, depth = lax.axis_size("row"), lax.axis_size("col"), lax.axis_size("dp")
    plane = rows * depth
    mine = lax.axis_index("row") * depth + lax.axis_index("dp")
    column = lax.axis_index("col")

    def in_plane(index):
        return {"row": index // depth, "dp": lax.rem(index, depth)}

    def in_column(index):
        return {"col": index}

    barrier = pltpu.get_barrier_semaphore()
    for me, count, peer in ((mine, plane, in_plane), (column, cols, in_column)):

        def signal(step, carry, me=me, count=count, peer=peer):
            to = peer(lax.rem(me + step, count))
            pl.semaphore_signal(barrier, inc=1, device_id=to, device_id_type=MESH)
            return carry

        lax.fori_loop(1, count, signal, 0)
    pl.semaphore_wait(barrier, plane + cols - 2)

    def run(me, count, peer, source, target, send, recv):
        def make(step, slot):
            to = lax.rem(me + step, count)
            return pltpu.make_async_remote_copy(
                src_ref=source(to),
                dst_ref=target(slot),
                send_sem=send.at[step],
                recv_sem=recv.at[slot],
                device_id=peer(to),
                device_id_type=MESH,
            )

        def start(step, carry):
            make(step, me).start()
            return carry

        def land(step, carry):
            make(step, me).wait_send()
            make(step, lax.rem(me + step, count)).wait_recv()
            return carry

        lax.fori_loop(1, count, start, 0)
        lax.fori_loop(1, count, land, 0)

    slots[mine] = x_ref[mine]
    run(mine, plane, in_plane, lambda to: x_ref.at[to], lambda at: slots.at[at], *sems[0:2])
    part[...] = jnp.sum(slots[...], axis=0)
    col_slots[column] = part[column]
    run(column, cols, in_column, lambda to: part.at[to], lambda at: col_slots.at[at], *sems[2:4])
    out_ref[mine, column] = jnp.sum(col_slots[...], axis=0)
    run(
        column, cols, in_column,
        lambda to: out_ref.at[mine, column], lambda at: out_ref.at[mine, at], *sems[4:6],
    )
    run(
        mine, plane, in_plane,
        lambda to: out_ref.at[mine], lambda at: out_ref.at[at], *sems[6:8],
    )


def grand_total(flat, number):
    cols = lax.axis_size("col")
    plane = lax.axis_size("row") * lax.axis_size("dp")
    count = plane * cols
    rows = flat.shape[0]
    each = -(-rows // (8 * count)) * 8
    padded = jnp.pad(flat, ((0, each * count - rows), (0, 0))).reshape(plane, cols, each, 128)
    out = pl.pallas_call(
        total_kernel,
        name="total",
        out_shape=shape(padded.shape, f32),
        in_specs=[vmem],
        out_specs=vmem,
        scratch_shapes=[
            pltpu.VMEM(padded.shape, f32),
            pltpu.VMEM(padded.shape[1:], f32),
            pltpu.VMEM(padded.shape[1:], f32),
        ]
        + [pltpu.SemaphoreType.DMA((plane,))] * 2
        + [pltpu.SemaphoreType.DMA((cols,))] * 4
        + [pltpu.SemaphoreType.DMA((plane,))] * 2,
        compiler_params=pltpu.CompilerParams(
            collective_id=number, has_side_effects=True, vmem_limit_bytes=LIMIT
        ),
    )(padded)
    return out.reshape(each * count, 128)[:rows]


def stack_shifts(centre, left, right, out_ref, dil):
    height, chans, side = centre.shape
    lane = lanes(chans, side)

    def body(row, carry):
        block, j = (row + reach) // 16, lax.rem(row + reach, 16)
        x = centre[row].astype(f32)
        low = pltpu.roll(left[block], lax.rem(dil - 8 - 8 * j + 2 * side, side), 1)
        high = pltpu.roll(right[block], lax.rem(2 * side - dil - 8 * j, side), 1)
        before = jnp.where(lane < dil, low, pltpu.roll(x, dil, 1))
        after = jnp.where(lane >= side - dil, high, pltpu.roll(x, side - dil, 1))
        out_ref[row] = jnp.concatenate(
            [before.astype(bf16), centre[row], after.astype(bf16)], axis=0
        )
        return carry

    lax.fori_loop(0, height, body, 0, unroll=4)


def taps_of(stack_ref, p, dil, group):
    return jnp.concatenate(
        [
            jnp.concatenate(
                [stack_ref[p + k + reach + u * dil] for k in range(group)], axis=1
            )
            for u in (-1, 0, 1)
        ],
        axis=0,
    )


def backward_kernel(
    meta, x_ref, top, bot, left, right, w_ref, out_ref, stack_ref, centre, low, high, *, length
):
    side = x_ref.shape[0]
    dil = meta[0]
    keep = [meta[k].astype(f32) for k in range(1, 5)]
    centre[pl.ds(reach, side)] = x_ref[...]
    centre[pl.ds(0, reach)] = (top[...].astype(f32) * keep[0]).astype(bf16)
    centre[pl.ds(reach + side, reach)] = (bot[...].astype(f32) * keep[1]).astype(bf16)
    blocks = left.shape[0]
    for k in range(blocks):
        edge = keep[0] if k == 0 else keep[1] if k == blocks - 1 else 1.0
        low[k] = left[k].astype(f32) * (keep[2] * edge)
        high[k] = right[k].astype(f32) * (keep[3] * edge)
    stack_shifts(centre, low, high, stack_ref, dil)

    def body(step, carry):
        p = 4 * step
        got = jnp.dot(w_ref[...], taps_of(stack_ref, p, dil, 4), preferred_element_type=f32)
        for k in range(4):
            out_ref[p + k] = got[:, side * k : side * (k + 1)] * (1.0 / length)
        return carry

    lax.fori_loop(0, side // 4, body, 0)


def moments(stat, count):
    mean = stat[:, 0:1] / count
    var = stat[:, 1:2] / count - mean * mean
    return mean, lax.rsqrt(var + eps)


def forward_kernel(
    meta, ids, x_ref, top, bot, left, right, stat, gain, bias, col_ids, w_ref,
    hid_ref, act_ref, slope_ref, sums_ref,
    centre_a, centre_s, low_a, high_a, low_s, high_s, *, count,
):
    side, chans = x_ref.shape[0], x_ref.shape[1]
    dil = meta[0]
    keep = [meta[k].astype(f32) for k in range(1, 5)]
    mean, scale = moments(stat[...], count)
    mean = jnp.broadcast_to(mean, (chans, side))
    scale = jnp.broadcast_to(scale, (chans, side))
    gained = jnp.broadcast_to(gain[...], (chans, side))

    def activate(x):
        norm = (x.astype(f32) - mean) * scale
        z = gained * norm
        e = jnp.exp(jnp.minimum(z, 0.0))
        return jnp.where(z > 0, z, e - 1.0), jnp.where(z > 0, 1.0, e) * norm

    def inner(p, carry):
        a, s = activate(x_ref[p])
        centre_a[p + reach] = a.astype(bf16)
        centre_s[p + reach] = s.astype(bf16)
        return carry

    lax.fori_loop(0, side, inner, 0, unroll=4)
    for k in range(reach):
        a, s = activate(top[k])
        centre_a[k] = (a * keep[0]).astype(bf16)
        centre_s[k] = (s * keep[0]).astype(bf16)
        a, s = activate(bot[k])
        centre_a[reach + side + k] = (a * keep[1]).astype(bf16)
        centre_s[reach + side + k] = (s * keep[1]).astype(bf16)
    blocks = left.shape[0]
    for k in range(blocks):
        edge = keep[0] if k == 0 else keep[1] if k == blocks - 1 else 1.0
        a, s = activate(left[k])
        low_a[k] = a * (keep[2] * edge)
        low_s[k] = s * (keep[2] * edge)
        a, s = activate(right[k])
        high_a[k] = a * (keep[3] * edge)
        high_s[k] = s * (keep[3] * edge)
    stack_shifts(centre_a, low_a, high_a, act_ref, dil)
    stack_shifts(centre_s, low_s, high_s, slope_ref, dil)
    biased = jnp.broadcast_to(bias[...], (chans, side))
    cols = jnp.broadcast_to(col_ids[...], (chans, side))

    def body(step, carry):
        one, two = carry
        p = 4 * step
        got = jnp.dot(w_ref[...], taps_of(act_ref, p, dil, 4), preferred_element_type=f32)
        for k in range(4):
            hid = got[:, side * k : side * (k + 1)] + jnp.where(cols != ids[p + k], biased, 0.0)
            hid_ref[p + k] = hid
            one = one + hid
            two = two + hid * hid
        return one, two

    zero = jnp.zeros((chans, side), f32)
    sums_ref[...] = as_columns(lax.fori_loop(0, side // 4, body, (zero, zero)), chans, side)


def second_kernel(
    meta, hid_ref, dact_ref, stat, gain, stack_ref, sums_ref, grad_ref, act_ref, *, count
):
    side, chans = hid_ref.shape[0], hid_ref.shape[1]
    dil = meta[0]
    mean, scale = moments(stat[...], count)
    mean = jnp.broadcast_to(mean, (chans, side))
    scale = jnp.broadcast_to(scale, (chans, side))
    gained = jnp.broadcast_to(gain[...], (chans, side))
    grad_ref[...] = jnp.zeros_like(grad_ref)

    def body(step, carry):
        sums = list(carry)
        p = 4 * step
        acts = []
        for k in range(4):
            dact = dact_ref[p + k]
            norm = (hid_ref[p + k] - mean) * scale
            z = gained * norm
            e = jnp.exp(jnp.minimum(z, 0.0))
            act = jnp.where(z > 0, z, e - 1.0).astype(bf16)
            acts.append(act)
            dz = dact * jnp.where(z > 0, 1.0, e)
            dn = gained * dz
            sums[0] = sums[0] + dn
            sums[1] = sums[1] + dn * norm
            sums[2] = sums[2] + dz * norm
            sums[3] = sums[3] + act.astype(f32) * dact
        grad_ref[...] += lax.dot_general(
            taps_of(stack_ref, p, dil, 4),
            jnp.concatenate(acts, axis=1),
            (((1,), (1,)), ((), ())),
            preferred_element_type=f32,
        )
        return tuple(sums)

    zero = jnp.zeros((chans, side), f32)
    sums = lax.fori_loop(0, side // 4, body, (zero,) * 4)
    sums_ref[...] = as_columns(sums, chans, side)


def first_kernel(
    meta, ids, hid_ref, dact_ref, stat, stat_two, gain, col_ids, act_ref, slope_ref, w_ref,
    sums_ref, grad_ref, slope_grad, *, count,
):
    side, chans = hid_ref.shape[0], hid_ref.shape[1]
    dil = meta[0]
    mean, scale = moments(stat[...], count)
    mean = jnp.broadcast_to(mean, (chans, side))
    scale = jnp.broadcast_to(scale, (chans, side))
    gained = jnp.broadcast_to(gain[...], (chans, side))
    mean_a = jnp.broadcast_to(stat_two[:, 0:1] / count, (chans, side))
    mean_b = jnp.broadcast_to(stat_two[:, 1:2] / count, (chans, side))
    cols = jnp.broadcast_to(col_ids[...], (chans, side))
    grad_ref[...] = jnp.zeros_like(grad_ref)
    slope_grad[...] = jnp.zeros_like(slope_grad)

    def body(step, total):
        p = 4 * step
        lows = []
        for k in range(4):
            norm = (hid_ref[p + k] - mean) * scale
            z = gained * norm
            slope = jnp.where(z > 0, 1.0, jnp.exp(jnp.minimum(z, 0.0)))
            dn = gained * (dact_ref[p + k] * slope)
            dhid = (dn - mean_a - norm * mean_b) * scale
            total = total + jnp.where(cols != ids[p + k], dhid, 0.0)
            lows.append(dhid.astype(bf16))
        low = jnp.concatenate(lows, axis=1)
        dims = (((1,), (1,)), ((), ()))
        grad_ref[...] += lax.dot_general(
            taps_of(act_ref, p, dil, 4), low, dims, preferred_element_type=f32
        )
        slope_grad[...] += lax.dot_general(
            taps_of(slope_ref, p, dil, 4), low, dims, preferred_element_type=f32
        )
        return total

    total = lax.fori_loop(0, side // 4, body, jnp.zeros((chans, side), f32))
    gain_grad = jnp.zeros((chans, chans), f32)
    for t in range(9):
        part = pl.ds(t * chans, chans)
        gain_grad = gain_grad + slope_grad[part, :] * w_ref[part, :]
    lane = lanes(chans, side)
    sums_ref[...] = jnp.where(
        lane == 1, jnp.sum(gain_grad, axis=1, keepdims=True), as_columns([total], chans, side)
    )


def compute(kernel, name, outs, specs, scratch=()):
    return pl.pallas_call(
        kernel,
        name=name,
        out_shape=outs,
        in_specs=specs,
        out_specs=jax.tree.map(lambda _: vmem, outs),
        scratch_shapes=list(scratch),
        compiler_params=pltpu.CompilerParams(vmem_limit_bytes=LIMIT),
    )


def local(pair, cotangent, chain, dilation, w_one, w_two, gain_one, gain_two, inter_bias):
    chans, side = pair.shape[1], pair.shape[2]
    rows, cols = lax.axis_size("row"), lax.axis_size("col")
    length = side * rows
    count = float(length * length)
    blocks = side // 16
    height = side + 2 * reach
    r, c = lax.axis_index("row"), lax.axis_index("col")

    cot = jnp.transpose(cotangent[0], (1, 0, 2))
    tile = jnp.transpose(pair[0], (1, 0, 2))

    keep = jnp.stack([r > 0, r < rows - 1, c > 0, c < cols - 1]).astype(jnp.int32)
    meta_one = jnp.concatenate([dilation[0:1], keep])
    meta_two = jnp.concatenate([dilation[1:2], keep])
    row_ids = lax.dynamic_slice_in_dim(chain[0], r * side, side)
    col_ids = lax.dynamic_slice_in_dim(chain[0], c * side, side)[None]
    gain_a, gain_b, bias = gain_one[:, None], gain_two[:, None], inter_bias[:, None]
    forward_w = jnp.transpose(w_one, (1, 0, 2)).reshape(chans, 9 * chans)
    backward_w = jnp.transpose(w_two[::-1], (2, 0, 1)).reshape(chans, 9 * chans)
    slope_w = jnp.transpose(w_one, (0, 2, 1)).reshape(9 * chans, chans).astype(f32)

    full = (side, chans, side)
    edge = shape((blocks, chans, side), bf16)
    stats = shape((chans, side), f32)
    stacked = shape((height, 3 * chans, side), bf16)
    centre = pltpu.VMEM((height, chans, side), bf16)
    border = pltpu.VMEM((blocks + 2, chans, side), f32)

    low, high = compute(edges_kernel, "edges", [edge, edge], [vmem])(cot)
    top, bot, left, right = halo(cot, low, high, 1)
    source, top = lax.optimization_barrier((pair[0], top))
    turned = jnp.transpose(source, (2, 0, 1))
    flip = 2 if rows % 4 == 0 else 1
    pairs = [(i, j) for i in range(rows) for j in range(cols)]
    aside = lax.ppermute(
        turned[side // 2 :],
        ("row", "col"),
        [(i * cols + j, (i ^ flip) * cols + j) for i, j in pairs],
    )
    direct = lax.ppermute(
        turned[: side // 2], ("row", "col"), [(i * cols + j, j * cols + i) for i, j in pairs]
    )
    d_act, cot_stack = compute(
        functools.partial(backward_kernel, length=length),
        "backward",
        [shape(full, f32), stacked],
        [smem] + [vmem] * 6,
        [centre, border, border],
    )(meta_two, cot, top, bot, left, right, backward_w)
    aside, d_act = lax.optimization_barrier((aside, d_act))
    onward = lax.ppermute(
        aside, ("row", "col"), [((i ^ flip) * cols + j, j * cols + i) for i, j in pairs]
    )

    sym, low, high, stat_one = compute(
        sym_kernel, "sym", [shape(full, bf16), edge, edge, stats], [vmem] * 4
    )(tile, direct, onward, cot)
    all_one, top, bot, left, right = border_stats(stat_one, sym, low, high, 2)
    hid, act_stack, slope_stack, stat_two = compute(
        functools.partial(forward_kernel, count=count),
        "forward",
        [shape(full, f32), stacked, stacked, stats],
        [smem, smem] + [vmem] * 10,
        [centre, centre, border, border, border, border],
    )(meta_one, row_ids, sym, top, bot, left, right, all_one, gain_a, bias, col_ids, forward_w)
    all_two = all_stats(stat_two, 4)
    stat_three, grad_two = compute(
        functools.partial(second_kernel, count=count),
        "second",
        [stats, shape((9 * chans, chans), f32)],
        [smem] + [vmem] * 5,
        [pltpu.VMEM((8, 128), f32)],
    )(meta_two, hid, d_act, all_two, gain_b, cot_stack)
    all_three = all_stats(stat_three, 5)
    stat_four, grad_one = compute(
        functools.partial(first_kernel, count=count),
        "first",
        [stats, shape((9 * chans, chans), f32)],
        [smem, smem] + [vmem] * 9,
        [pltpu.VMEM((9 * chans, chans), f32)],
    )(
        meta_one, row_ids, hid, d_act, all_two, all_three, gain_b, col_ids, act_stack,
        slope_stack, slope_w,
    )

    loss = stat_one[:, 2] * (1.0 / length) + stat_three[:, 3]
    vectors = jnp.stack([stat_four[:, 1], stat_three[:, 2], stat_four[:, 0], loss])
    flat = jnp.concatenate(
        [grad_one.reshape(-1, 128), grad_two.reshape(-1, 128), vectors.reshape(-1, 128)]
    )
    total = grand_total(flat, 6)
    size = 9 * chans * chans // 128
    out_one = jnp.transpose(total[:size].reshape(9, chans, chans), (0, 2, 1))
    out_two = total[size : 2 * size].reshape(9, chans, chans)[::-1] * (1.0 / length)
    ends = total[2 * size :].reshape(4, chans)
    return out_one, out_two, ends[0], ends[1], ends[2], jnp.sum(ends[3])


def solution(mesh):
    in_specs = (
        P("dp", None, "row", "col"),
        P("dp", None, "row", "col"),
        P("dp", None),
        P(),
        P(),
        P(),
        P(),
        P(),
        P(),
    )
    out_specs = (P(), P(), P(), P(), P(), P())
    return jax.shard_map(local, mesh=mesh, in_specs=in_specs, out_specs=out_specs, check_vma=False)
```

```python
import functools

import jax
import jax.numpy as jnp
from jax import lax
from jax.experimental import pallas as pl
from jax.experimental.pallas import tpu as pltpu
from jax.sharding import PartitionSpec as P

reach = 8
group = 8
eps = 1e-05
f32 = jnp.float32
bf16 = jnp.bfloat16
MESH = pl.DeviceIdType.MESH
vmem = pl.BlockSpec(memory_space=pltpu.VMEM)
smem = pl.BlockSpec(memory_space=pltpu.SMEM)
anyspace = pl.BlockSpec(memory_space=pl.ANY)
LIMIT = 56 * 1024 * 1024


def shape(dims, dtype):
    return jax.ShapeDtypeStruct(dims, dtype)


def lanes(chans=64, width=128):
    return lax.broadcasted_iota(jnp.int32, (chans, width), 1)


def pack_edges(rows, chans, side):
    group = lanes(chans, side) // reach
    low = jnp.zeros((chans, side), f32)
    high = jnp.zeros((chans, side), f32)
    for j, row in enumerate(rows):
        low = jnp.where(group == j, row if j == 0 else pltpu.roll(row, 8 * j, 1), low)
        shift = (8 * j + 8) % side
        high = jnp.where(group == j, row if shift == 0 else pltpu.roll(row, shift, 1), high)
    return low.astype(bf16), high.astype(bf16)


def as_columns(columns, chans, side):
    lane = lanes(chans, side)
    tile = jnp.zeros((chans, side), f32)
    for k, values in enumerate(columns):
        tile = jnp.where(lane == k, jnp.sum(values, axis=1, keepdims=True), tile)
    return tile


def edges_kernel(x_ref, low_ref, high_ref):
    side, chans = x_ref.shape[0], x_ref.shape[1]

    def body(k, carry):
        rows = [x_ref[16 * k + j].astype(f32) for j in range(16)]
        low_ref[k], high_ref[k] = pack_edges(rows, chans, side)
        return carry

    lax.fori_loop(0, side // 16, body, 0)


def sym_kernel(x_ref, first_ref, last_ref, cot_ref, sym_ref, low_ref, high_ref, stat_ref):
    side, chans = x_ref.shape[0], x_ref.shape[1]
    half = side // 2

    def body(m_ref, base, k, carry):
        one, two, three = carry
        rows = []
        for j in range(16):
            p = 16 * k + j
            sym = ((x_ref[p + base].astype(f32) + m_ref[p].astype(f32)) * 0.5).astype(bf16)
            sym_ref[p + base] = sym
            wide = sym.astype(f32)
            rows.append(wide)
            one = one + wide
            two = two + wide * wide
            three = three + wide * cot_ref[p + base].astype(f32)
        at = k + base // 16
        low_ref[at], high_ref[at] = pack_edges(rows, chans, side)
        return one, two, three

    zero = jnp.zeros((chans, side), f32)
    sums = (zero, zero, zero)
    for m_ref, base in ((first_ref, 0), (last_ref, half)):
        sums = lax.fori_loop(0, half // 16, functools.partial(body, m_ref, base), sums)
    stat_ref[...] = as_columns(sums, chans, side)


def halo_body(x_ref, low_ref, high_ref, top_ref, bot_ref, left_ref, right_ref, send, recv):
    rows, cols = lax.axis_size("row"), lax.axis_size("col")
    r, c = lax.axis_index("row"), lax.axis_index("col")
    up, down = lax.rem(r + rows - 1, rows), lax.rem(r + 1, rows)
    lef, rig = lax.rem(c + cols - 1, cols), lax.rem(c + 1, cols)
    side, blocks = x_ref.shape[0], low_ref.shape[0]
    moves = [
        (high_ref, left_ref.at[pl.ds(1, blocks)], r, rig),
        (low_ref, right_ref.at[pl.ds(1, blocks)], r, lef),
        (x_ref.at[pl.ds(side - reach, reach)], top_ref, down, c),
        (x_ref.at[pl.ds(0, reach)], bot_ref, up, c),
        (high_ref.at[pl.ds(blocks - 1, 1)], left_ref.at[pl.ds(0, 1)], down, rig),
        (high_ref.at[pl.ds(0, 1)], left_ref.at[pl.ds(blocks + 1, 1)], up, rig),
        (low_ref.at[pl.ds(blocks - 1, 1)], right_ref.at[pl.ds(0, 1)], down, lef),
        (low_ref.at[pl.ds(0, 1)], right_ref.at[pl.ds(blocks + 1, 1)], up, lef),
    ]
    return [
        pltpu.make_async_remote_copy(
            src_ref=src,
            dst_ref=dst,
            send_sem=send.at[n],
            recv_sem=recv.at[n],
            device_id={"row": to_row, "col": to_col},
            device_id_type=MESH,
        )
        for n, (src, dst, to_row, to_col) in enumerate(moves)
    ]


def halo_kernel(x_ref, low_ref, high_ref, top_ref, bot_ref, left_ref, right_ref, send, recv):
    rows, cols = lax.axis_size("row"), lax.axis_size("col")
    r, c = lax.axis_index("row"), lax.axis_index("col")
    barrier = pltpu.get_barrier_semaphore()
    for a in (-1, 0, 1):
        for b in (-1, 0, 1):
            if a or b:
                pl.semaphore_signal(
                    barrier,
                    inc=1,
                    device_id={
                        "row": lax.rem(r + rows + a, rows),
                        "col": lax.rem(c + cols + b, cols),
                    },
                    device_id_type=MESH,
                )
    pl.semaphore_wait(barrier, 8)
    copies = halo_body(x_ref, low_ref, high_ref, top_ref, bot_ref, left_ref, right_ref, send, recv)
    for copy in copies:
        copy.start()
    for copy in copies:
        copy.wait()


def halo(x, low, high, number):
    side, chans, width = x.shape
    blocks = low.shape[0]
    return pl.pallas_call(
        halo_kernel,
        name="halo",
        out_shape=[
            shape((reach, chans, width), bf16),
            shape((reach, chans, width), bf16),
            shape((blocks + 2, chans, width), bf16),
            shape((blocks + 2, chans, width), bf16),
        ],
        in_specs=[anyspace] * 3,
        out_specs=[anyspace] * 4,
        scratch_shapes=[pltpu.SemaphoreType.DMA((8,)), pltpu.SemaphoreType.DMA((8,))],
        compiler_params=pltpu.CompilerParams(collective_id=number, has_side_effects=True),
    )(x, low, high)


def greet(barrier, me, count, peer):
    def body(step, carry):
        to = lax.rem(me + step, count)
        pl.semaphore_signal(barrier, inc=1, device_id=peer(to), device_id_type=MESH)
        return carry

    lax.fori_loop(1, count, body, 0)
    pl.semaphore_wait(barrier, count - 1)


def stats_kernel(x_ref, out_ref, own, slots, send, recv):
    rows, cols = lax.axis_size("row"), lax.axis_size("col")
    count = rows * cols
    me = lax.axis_index("row") * cols + lax.axis_index("col")
    chans = x_ref.shape[0]

    def peer(index):
        return {"row": index // cols, "col": lax.rem(index, cols)}

    greet(pltpu.get_barrier_semaphore(), me, count, peer)
    own[...] = x_ref[...].T[0:8, :]

    def copy_to(step):
        return pltpu.make_async_remote_copy(
            src_ref=own,
            dst_ref=slots.at[me],
            send_sem=send.at[step],
            recv_sem=recv.at[me],
            device_id=peer(lax.rem(me + step, count)),
            device_id_type=MESH,
        )

    def copy_from(step):
        source = lax.rem(me + step, count)
        return pltpu.make_async_remote_copy(
            src_ref=own,
            dst_ref=slots.at[source],
            send_sem=send.at[step],
            recv_sem=recv.at[source],
            device_id=peer(source),
            device_id_type=MESH,
        )

    def start(step, carry):
        copy_to(step).start()
        return carry

    def land(step, carry):
        copy_to(step).wait_send()
        copy_from(step).wait_recv()
        return carry

    slots[me] = own[...]
    lax.fori_loop(1, count, start, 0)
    lax.fori_loop(1, count, land, 0)
    total = jnp.sum(slots[...], axis=0)
    filled = jnp.concatenate([total, jnp.zeros((x_ref.shape[1] - 8, chans), f32)], axis=0)
    out_ref[...] = filled.T


def border_stats_kernel(
    tile_ref, x_ref, low_ref, high_ref, out_ref, top_ref, bot_ref, left_ref, right_ref,
    own, slots, send, recv, halo_send, halo_recv,
):
    rows, cols = lax.axis_size("row"), lax.axis_size("col")
    count = rows * cols
    me = lax.axis_index("row") * cols + lax.axis_index("col")
    chans = tile_ref.shape[0]

    def peer(index):
        return {"row": index // cols, "col": lax.rem(index, cols)}

    greet(pltpu.get_barrier_semaphore(), me, count, peer)
    copies = halo_body(
        x_ref, low_ref, high_ref, top_ref, bot_ref, left_ref, right_ref, halo_send, halo_recv
    )
    for copy in copies:
        copy.start()
    own[...] = tile_ref[...].T[0:8, :]

    def copy_of(step, slot):
        return pltpu.make_async_remote_copy(
            src_ref=own,
            dst_ref=slots.at[slot],
            send_sem=send.at[step],
            recv_sem=recv.at[slot],
            device_id=peer(lax.rem(me + step, count)),
            device_id_type=MESH,
        )

    def start(step, carry):
        copy_of(step, me).start()
        return carry

    def land(step, carry):
        copy_of(step, me).wait_send()
        copy_of(step, lax.rem(me + step, count)).wait_recv()
        return carry

    slots[me] = own[...]
    lax.fori_loop(1, count, start, 0)
    lax.fori_loop(1, count, land, 0)
    total = jnp.sum(slots[...], axis=0)
    filled = jnp.concatenate([total, jnp.zeros((tile_ref.shape[1] - 8, chans), f32)], axis=0)
    out_ref[...] = filled.T
    for copy in copies:
        copy.wait()


def border_stats(tile, x, low, high, number):
    side, chans, width = x.shape
    blocks = low.shape[0]
    count = lax.axis_size("row") * lax.axis_size("col")
    return pl.pallas_call(
        border_stats_kernel,
        name="border_stats",
        out_shape=[
            shape(tile.shape, f32),
            shape((reach, chans, width), bf16),
            shape((reach, chans, width), bf16),
            shape((blocks + 2, chans, width), bf16),
            shape((blocks + 2, chans, width), bf16),
        ],
        in_specs=[vmem] + [anyspace] * 3,
        out_specs=[vmem] + [anyspace] * 4,
        scratch_shapes=[
            pltpu.VMEM((8, chans), f32),
            pltpu.VMEM((count, 8, chans), f32),
            pltpu.SemaphoreType.DMA((count,)),
            pltpu.SemaphoreType.DMA((count,)),
            pltpu.SemaphoreType.DMA((8,)),
            pltpu.SemaphoreType.DMA((8,)),
        ],
        compiler_params=pltpu.CompilerParams(collective_id=number, has_side_effects=True),
    )(tile, x, low, high)


def all_stats(tile, number):
    count = lax.axis_size("row") * lax.axis_size("col")
    chans = tile.shape[0]
    return pl.pallas_call(
        stats_kernel,
        name="stats",
        out_shape=shape(tile.shape, f32),
        in_specs=[vmem],
        out_specs=vmem,
        scratch_shapes=[
            pltpu.VMEM((8, chans), f32),
            pltpu.VMEM((count, 8, chans), f32),
            pltpu.SemaphoreType.DMA((count,)),
            pltpu.SemaphoreType.DMA((count,)),
        ],
        compiler_params=pltpu.CompilerParams(collective_id=number, has_side_effects=True),
    )(tile)


def total_kernel(x_ref, out_ref, slots, part, col_slots, *sems):
    rows, cols, depth = lax.axis_size("row"), lax.axis_size("col"), lax.axis_size("dp")
    plane = rows * depth
    mine = lax.axis_index("row") * depth + lax.axis_index("dp")
    column = lax.axis_index("col")

    def in_plane(index):
        return {"row": index // depth, "dp": lax.rem(index, depth)}

    def in_column(index):
        return {"col": index}

    barrier = pltpu.get_barrier_semaphore()
    for me, count, peer in ((mine, plane, in_plane), (column, cols, in_column)):

        def signal(step, carry, me=me, count=count, peer=peer):
            to = peer(lax.rem(me + step, count))
            pl.semaphore_signal(barrier, inc=1, device_id=to, device_id_type=MESH)
            return carry

        lax.fori_loop(1, count, signal, 0)
    pl.semaphore_wait(barrier, plane + cols - 2)

    def run(me, count, peer, source, target, send, recv):
        def make(step, slot):
            to = lax.rem(me + step, count)
            return pltpu.make_async_remote_copy(
                src_ref=source(to),
                dst_ref=target(slot),
                send_sem=send.at[step],
                recv_sem=recv.at[slot],
                device_id=peer(to),
                device_id_type=MESH,
            )

        def start(step, carry):
            make(step, me).start()
            return carry

        def land(step, carry):
            make(step, me).wait_send()
            make(step, lax.rem(me + step, count)).wait_recv()
            return carry

        lax.fori_loop(1, count, start, 0)
        lax.fori_loop(1, count, land, 0)

    slots[mine] = x_ref[mine]
    run(mine, plane, in_plane, lambda to: x_ref.at[to], lambda at: slots.at[at], *sems[0:2])
    part[...] = jnp.sum(slots[...], axis=0)
    col_slots[column] = part[column]
    run(column, cols, in_column, lambda to: part.at[to], lambda at: col_slots.at[at], *sems[2:4])
    out_ref[mine, column] = jnp.sum(col_slots[...], axis=0)
    run(
        column, cols, in_column,
        lambda to: out_ref.at[mine, column], lambda at: out_ref.at[mine, at], *sems[4:6],
    )
    run(
        mine, plane, in_plane,
        lambda to: out_ref.at[mine], lambda at: out_ref.at[at], *sems[6:8],
    )


def grand_total(flat, number):
    cols = lax.axis_size("col")
    plane = lax.axis_size("row") * lax.axis_size("dp")
    count = plane * cols
    rows = flat.shape[0]
    each = -(-rows // (8 * count)) * 8
    padded = jnp.pad(flat, ((0, each * count - rows), (0, 0))).reshape(plane, cols, each, 128)
    out = pl.pallas_call(
        total_kernel,
        name="total",
        out_shape=shape(padded.shape, f32),
        in_specs=[vmem],
        out_specs=vmem,
        scratch_shapes=[
            pltpu.VMEM(padded.shape, f32),
            pltpu.VMEM(padded.shape[1:], f32),
            pltpu.VMEM(padded.shape[1:], f32),
        ]
        + [pltpu.SemaphoreType.DMA((plane,))] * 2
        + [pltpu.SemaphoreType.DMA((cols,))] * 4
        + [pltpu.SemaphoreType.DMA((plane,))] * 2,
        compiler_params=pltpu.CompilerParams(
            collective_id=number, has_side_effects=True, vmem_limit_bytes=LIMIT
        ),
    )(padded)
    return out.reshape(each * count, 128)[:rows]


def stack_shifts(centre, left, right, out_ref, dil):
    height, chans, side = centre.shape
    lane = lanes(chans, side)

    def body(row, carry):
        block, j = (row + reach) // 16, lax.rem(row + reach, 16)
        x = centre[row].astype(f32)
        low = pltpu.roll(left[block], lax.rem(dil - 8 - 8 * j + 2 * side, side), 1)
        high = pltpu.roll(right[block], lax.rem(2 * side - dil - 8 * j, side), 1)
        before = jnp.where(lane < dil, low, pltpu.roll(x, dil, 1))
        after = jnp.where(lane >= side - dil, high, pltpu.roll(x, side - dil, 1))
        out_ref[row] = jnp.concatenate(
            [before.astype(bf16), centre[row], after.astype(bf16)], axis=0
        )
        return carry

    lax.fori_loop(0, height, body, 0, unroll=4)


def taps_of(stack_ref, p, dil, group):
    return jnp.concatenate(
        [
            jnp.concatenate(
                [stack_ref[p + k + reach + u * dil] for k in range(group)], axis=1
            )
            for u in (-1, 0, 1)
        ],
        axis=0,
    )


def backward_kernel(
    meta, x_ref, top, bot, left, right, w_ref, out_ref, stack_ref, centre, low, high, *, length
):
    side = x_ref.shape[0]
    dil = meta[0]
    keep = [meta[k].astype(f32) for k in range(1, 5)]
    centre[pl.ds(reach, side)] = x_ref[...]
    centre[pl.ds(0, reach)] = (top[...].astype(f32) * keep[0]).astype(bf16)
    centre[pl.ds(reach + side, reach)] = (bot[...].astype(f32) * keep[1]).astype(bf16)
    blocks = left.shape[0]
    for k in range(blocks):
        edge = keep[0] if k == 0 else keep[1] if k == blocks - 1 else 1.0
        low[k] = left[k].astype(f32) * (keep[2] * edge)
        high[k] = right[k].astype(f32) * (keep[3] * edge)
    stack_shifts(centre, low, high, stack_ref, dil)

    def body(step, carry):
        p = group * step
        got = jnp.dot(w_ref[...], taps_of(stack_ref, p, dil, group), preferred_element_type=f32)
        for k in range(group):
            out_ref[p + k] = got[:, side * k : side * (k + 1)] * (1.0 / length)
        return carry

    lax.fori_loop(0, side // group, body, 0)


def moments(stat, count):
    mean = stat[:, 0:1] / count
    var = stat[:, 1:2] / count - mean * mean
    return mean, lax.rsqrt(var + eps)


def forward_kernel(
    meta, ids, x_ref, top, bot, left, right, stat, gain, bias, col_ids, w_ref,
    hid_ref, act_ref, slope_ref, sums_ref,
    centre_a, centre_s, low_a, high_a, low_s, high_s, *, count,
):
    side, chans = x_ref.shape[0], x_ref.shape[1]
    dil = meta[0]
    keep = [meta[k].astype(f32) for k in range(1, 5)]
    mean, scale = moments(stat[...], count)
    mean = jnp.broadcast_to(mean, (chans, side))
    scale = jnp.broadcast_to(scale, (chans, side))
    gained = jnp.broadcast_to(gain[...], (chans, side))

    def activate(x):
        norm = (x.astype(f32) - mean) * scale
        z = gained * norm
        e = jnp.exp(jnp.minimum(z, 0.0))
        return jnp.where(z > 0, z, e - 1.0), jnp.where(z > 0, 1.0, e) * norm

    def inner(p, carry):
        a, s = activate(x_ref[p])
        centre_a[p + reach] = a.astype(bf16)
        centre_s[p + reach] = s.astype(bf16)
        return carry

    lax.fori_loop(0, side, inner, 0, unroll=4)
    for k in range(reach):
        a, s = activate(top[k])
        centre_a[k] = (a * keep[0]).astype(bf16)
        centre_s[k] = (s * keep[0]).astype(bf16)
        a, s = activate(bot[k])
        centre_a[reach + side + k] = (a * keep[1]).astype(bf16)
        centre_s[reach + side + k] = (s * keep[1]).astype(bf16)
    blocks = left.shape[0]
    for k in range(blocks):
        edge = keep[0] if k == 0 else keep[1] if k == blocks - 1 else 1.0
        a, s = activate(left[k])
        low_a[k] = a * (keep[2] * edge)
        low_s[k] = s * (keep[2] * edge)
        a, s = activate(right[k])
        high_a[k] = a * (keep[3] * edge)
        high_s[k] = s * (keep[3] * edge)
    stack_shifts(centre_a, low_a, high_a, act_ref, dil)
    stack_shifts(centre_s, low_s, high_s, slope_ref, dil)
    biased = jnp.broadcast_to(bias[...], (chans, side))
    cols = jnp.broadcast_to(col_ids[...], (chans, side))

    def body(step, carry):
        one, two = carry
        p = group * step
        got = jnp.dot(w_ref[...], taps_of(act_ref, p, dil, group), preferred_element_type=f32)
        for k in range(group):
            hid = got[:, side * k : side * (k + 1)] + jnp.where(cols != ids[p + k], biased, 0.0)
            hid_ref[p + k] = hid
            one = one + hid
            two = two + hid * hid
        return one, two

    zero = jnp.zeros((chans, side), f32)
    sums_ref[...] = as_columns(lax.fori_loop(0, side // group, body, (zero, zero)), chans, side)


def second_kernel(
    meta, hid_ref, dact_ref, stat, gain, stack_ref, sums_ref, grad_ref, act_ref, *, count
):
    side, chans = hid_ref.shape[0], hid_ref.shape[1]
    dil = meta[0]
    mean, scale = moments(stat[...], count)
    mean = jnp.broadcast_to(mean, (chans, side))
    scale = jnp.broadcast_to(scale, (chans, side))
    gained = jnp.broadcast_to(gain[...], (chans, side))
    grad_ref[...] = jnp.zeros_like(grad_ref)

    def body(step, carry):
        sums = list(carry)
        p = group * step
        acts = []
        for k in range(group):
            dact = dact_ref[p + k]
            norm = (hid_ref[p + k] - mean) * scale
            z = gained * norm
            e = jnp.exp(jnp.minimum(z, 0.0))
            act = jnp.where(z > 0, z, e - 1.0).astype(bf16)
            acts.append(act)
            dz = dact * jnp.where(z > 0, 1.0, e)
            dn = gained * dz
            sums[0] = sums[0] + dn
            sums[1] = sums[1] + dn * norm
            sums[2] = sums[2] + dz * norm
            sums[3] = sums[3] + act.astype(f32) * dact
        grad_ref[...] += lax.dot_general(
            taps_of(stack_ref, p, dil, group),
            jnp.concatenate(acts, axis=1),
            (((1,), (1,)), ((), ())),
            preferred_element_type=f32,
        )
        return tuple(sums)

    zero = jnp.zeros((chans, side), f32)
    sums = lax.fori_loop(0, side // group, body, (zero,) * 4)
    sums_ref[...] = as_columns(sums, chans, side)


def first_kernel(
    meta, ids, hid_ref, dact_ref, stat, stat_two, gain, col_ids, act_ref, slope_ref, w_ref,
    sums_ref, grad_ref, slope_grad, *, count,
):
    side, chans = hid_ref.shape[0], hid_ref.shape[1]
    dil = meta[0]
    mean, scale = moments(stat[...], count)
    mean = jnp.broadcast_to(mean, (chans, side))
    scale = jnp.broadcast_to(scale, (chans, side))
    gained = jnp.broadcast_to(gain[...], (chans, side))
    mean_a = jnp.broadcast_to(stat_two[:, 0:1] / count, (chans, side))
    mean_b = jnp.broadcast_to(stat_two[:, 1:2] / count, (chans, side))
    cols = jnp.broadcast_to(col_ids[...], (chans, side))
    grad_ref[...] = jnp.zeros_like(grad_ref)
    slope_grad[...] = jnp.zeros_like(slope_grad)

    def body(step, total):
        p = group * step
        lows = []
        for k in range(group):
            norm = (hid_ref[p + k] - mean) * scale
            z = gained * norm
            slope = jnp.where(z > 0, 1.0, jnp.exp(jnp.minimum(z, 0.0)))
            dn = gained * (dact_ref[p + k] * slope)
            dhid = (dn - mean_a - norm * mean_b) * scale
            total = total + jnp.where(cols != ids[p + k], dhid, 0.0)
            lows.append(dhid.astype(bf16))
        low = jnp.concatenate(lows, axis=1)
        dims = (((1,), (1,)), ((), ()))
        grad_ref[...] += lax.dot_general(
            taps_of(act_ref, p, dil, group), low, dims, preferred_element_type=f32
        )
        slope_grad[...] += lax.dot_general(
            taps_of(slope_ref, p, dil, group), low, dims, preferred_element_type=f32
        )
        return total

    total = lax.fori_loop(0, side // group, body, jnp.zeros((chans, side), f32))
    gain_grad = jnp.zeros((chans, chans), f32)
    for t in range(9):
        part = pl.ds(t * chans, chans)
        gain_grad = gain_grad + slope_grad[part, :] * w_ref[part, :]
    lane = lanes(chans, side)
    sums_ref[...] = jnp.where(
        lane == 1, jnp.sum(gain_grad, axis=1, keepdims=True), as_columns([total], chans, side)
    )


def compute(kernel, name, outs, specs, scratch=()):
    return pl.pallas_call(
        kernel,
        name=name,
        out_shape=outs,
        in_specs=specs,
        out_specs=jax.tree.map(lambda _: vmem, outs),
        scratch_shapes=list(scratch),
        compiler_params=pltpu.CompilerParams(vmem_limit_bytes=LIMIT),
    )


def local(pair, cotangent, chain, dilation, w_one, w_two, gain_one, gain_two, inter_bias):
    chans, side = pair.shape[1], pair.shape[2]
    rows, cols = lax.axis_size("row"), lax.axis_size("col")
    length = side * rows
    count = float(length * length)
    blocks = side // 16
    height = side + 2 * reach
    r, c = lax.axis_index("row"), lax.axis_index("col")

    cot = jnp.transpose(cotangent[0], (1, 0, 2))
    tile = jnp.transpose(pair[0], (1, 0, 2))

    keep = jnp.stack([r > 0, r < rows - 1, c > 0, c < cols - 1]).astype(jnp.int32)
    meta_one = jnp.concatenate([dilation[0:1], keep])
    meta_two = jnp.concatenate([dilation[1:2], keep])
    row_ids = lax.dynamic_slice_in_dim(chain[0], r * side, side)
    col_ids = lax.dynamic_slice_in_dim(chain[0], c * side, side)[None]
    gain_a, gain_b, bias = gain_one[:, None], gain_two[:, None], inter_bias[:, None]
    forward_w = jnp.transpose(w_one, (1, 0, 2)).reshape(chans, 9 * chans)
    backward_w = jnp.transpose(w_two[::-1], (2, 0, 1)).reshape(chans, 9 * chans)
    slope_w = jnp.transpose(w_one, (0, 2, 1)).reshape(9 * chans, chans).astype(f32)

    full = (side, chans, side)
    edge = shape((blocks, chans, side), bf16)
    stats = shape((chans, side), f32)
    stacked = shape((height, 3 * chans, side), bf16)
    centre = pltpu.VMEM((height, chans, side), bf16)
    border = pltpu.VMEM((blocks + 2, chans, side), f32)

    low, high = compute(edges_kernel, "edges", [edge, edge], [vmem])(cot)
    top, bot, left, right = halo(cot, low, high, 1)
    source, top = lax.optimization_barrier((pair[0], top))
    turned = jnp.transpose(source, (2, 0, 1))
    flip = 2 if rows % 4 == 0 else 1
    pairs = [(i, j) for i in range(rows) for j in range(cols)]
    aside = lax.ppermute(
        turned[side // 2 :],
        ("row", "col"),
        [(i * cols + j, (i ^ flip) * cols + j) for i, j in pairs],
    )
    direct = lax.ppermute(
        turned[: side // 2], ("row", "col"), [(i * cols + j, j * cols + i) for i, j in pairs]
    )
    d_act, cot_stack = compute(
        functools.partial(backward_kernel, length=length),
        "backward",
        [shape(full, f32), stacked],
        [smem] + [vmem] * 6,
        [centre, border, border],
    )(meta_two, cot, top, bot, left, right, backward_w)
    aside, d_act = lax.optimization_barrier((aside, d_act))
    onward = lax.ppermute(
        aside, ("row", "col"), [((i ^ flip) * cols + j, j * cols + i) for i, j in pairs]
    )

    sym, low, high, stat_one = compute(
        sym_kernel, "sym", [shape(full, bf16), edge, edge, stats], [vmem] * 4
    )(tile, direct, onward, cot)
    all_one, top, bot, left, right = border_stats(stat_one, sym, low, high, 2)
    hid, act_stack, slope_stack, stat_two = compute(
        functools.partial(forward_kernel, count=count),
        "forward",
        [shape(full, f32), stacked, stacked, stats],
        [smem, smem] + [vmem] * 10,
        [centre, centre, border, border, border, border],
    )(meta_one, row_ids, sym, top, bot, left, right, all_one, gain_a, bias, col_ids, forward_w)
    all_two = all_stats(stat_two, 4)
    stat_three, grad_two = compute(
        functools.partial(second_kernel, count=count),
        "second",
        [stats, shape((9 * chans, chans), f32)],
        [smem] + [vmem] * 5,
        [pltpu.VMEM((8, 128), f32)],
    )(meta_two, hid, d_act, all_two, gain_b, cot_stack)
    all_three = all_stats(stat_three, 5)
    stat_four, grad_one = compute(
        functools.partial(first_kernel, count=count),
        "first",
        [stats, shape((9 * chans, chans), f32)],
        [smem, smem] + [vmem] * 9,
        [pltpu.VMEM((9 * chans, chans), f32)],
    )(
        meta_one, row_ids, hid, d_act, all_two, all_three, gain_b, col_ids, act_stack,
        slope_stack, slope_w,
    )

    loss = stat_one[:, 2] * (1.0 / length) + stat_three[:, 3]
    vectors = jnp.stack([stat_four[:, 1], stat_three[:, 2], stat_four[:, 0], loss])
    flat = jnp.concatenate(
        [grad_one.reshape(-1, 128), grad_two.reshape(-1, 128), vectors.reshape(-1, 128)]
    )
    total = grand_total(flat, 6)
    size = 9 * chans * chans // 128
    out_one = jnp.transpose(total[:size].reshape(9, chans, chans), (0, 2, 1))
    out_two = total[size : 2 * size].reshape(9, chans, chans)[::-1] * (1.0 / length)
    ends = total[2 * size :].reshape(4, chans)
    return out_one, out_two, ends[0], ends[1], ends[2], jnp.sum(ends[3])


def solution(mesh):
    in_specs = (
        P("dp", None, "row", "col"),
        P("dp", None, "row", "col"),
        P("dp", None),
        P(),
        P(),
        P(),
        P(),
        P(),
        P(),
    )
    out_specs = (P(), P(), P(), P(), P(), P())
    return jax.shard_map(local, mesh=mesh, in_specs=in_specs, out_specs=out_specs, check_vma=False)
```
